256 devices in a mesh: cp: 64 (over z_hi, x, y), blk: 4 (over z_lo, core).
Axes of the slice: x: 4, y: 4, z: 8 (z_hi: 4, z_lo: 2; z = z_hi * 2 + z_lo), core: 2. Of those that a mesh axis runs over, the one named last changes fastest.
Arguments:
- queries: bfloat16 [16384, 3072], P(('cp', 'blk')), may hold values from -8 to 8
- key_vectors: bfloat16 [16384, 512], P(('cp', 'blk')), may hold values from -8 to 8
- value_vectors: bfloat16 [16384, 512], P(('cp', 'blk')), may hold values from -6 to 6
- segment_lengths: int32 [16], replicated, may hold values from 1 to 2048, 16384 in all
- segment_allowed: int32 [16, 16], replicated, may hold values from 0 to 1, as said below
- noise_level: int32 [16], replicated, may hold values from 0 to 15
- gate_table: bfloat16 [16, 3072], P(None, 'blk'), may hold values from 0.099609375 to 1.8984375
Outputs:
- attended: bfloat16 [16384, 3072], P(('cp', 'blk'))
The draws below stay inside these ranges and needn't reach their ends.
Inputs may be any that keep to these rules, and one draw needn't show every extreme that they name: `segment_lengths`: the longest segment has exactly 2048 tokens. segment_allowed[a, b] is 0 for b > a, 1 for b = a and for b = 0, either value otherwise.
All inputs are finite; a program needn't handle non-finite values.
Results may differ from the reference program's by a relative error of at most 0.0055.
Values may be sent and summed in bfloat16 or wider, within the bound.
No kernel may reach another device: no remote copies, remote signals or barrier semaphores. Data moves between devices by JAX's collectives and lax.ppermute only.
A program may use at most 64 MiB of HBM per device.

```python
import math
import jax
import jax.numpy as jnp
import numpy as np
from jax import lax

HEADS = 24
KV_HEADS = 4
HEAD_DIM = 128
SEGMENTS = 16
LEVELS = 16
SEQ = 16384
MOST = 2048


def draw_queries(key, part):
    key = jax.random.fold_in(key, 11)
    first_key = jax.random.fold_in(key, 0)
    noise = jnp.clip(jax.random.normal(first_key, (SEQ, HEADS * HEAD_DIM), jnp.float32) * 1.6, -8.0, 8.0)
    return noise.astype(jnp.bfloat16)


def draw_key_vectors(key, part):
    key = jax.random.fold_in(key, 13)
    first_key = jax.random.fold_in(key, 0)
    noise = jnp.clip(jax.random.normal(first_key, (SEQ, KV_HEADS * HEAD_DIM), jnp.float32) * 1.6, -8.0, 8.0)
    return noise.astype(jnp.bfloat16)


def draw_segment_allowed(key, part):
    key = jax.random.fold_in(key, 7)
    picks = jax.random.randint(key, (SEGMENTS, SEGMENTS), 0, 10)
    query_segment = jnp.arange(SEGMENTS, dtype=jnp.int32)[:, None]
    key_segment = jnp.arange(SEGMENTS, dtype=jnp.int32)[None, :]
    chosen = jnp.where(picks < 6, 1, 0)
    chosen = jnp.where((key_segment == query_segment) | (key_segment == 0), 1, chosen)
    return jnp.where(key_segment > query_segment, 0, chosen).astype(jnp.int32)


def touch_ends(values, own_key, low, largest):
    dims = values.shape
    place = [jax.random.randint(jax.random.fold_in(own_key, axis), (), 0, dims[axis]) for axis in range(len(dims))]
    values = values.at[tuple(place)].set(low)
    longest = dims.index(max(dims))
    place[longest] = (place[longest] + 1) % dims[longest]
    return values.at[tuple(place)].set(largest)


def block_levels(stream_key, extent, shards, least, largest):
    factor_of, own = 1.0, jax.random.fold_in(stream_key, 6)
    for dim, shards_of in shards:
        draws = jnp.exp(jax.random.uniform(jax.random.fold_in(own, dim), (shards_of,), jnp.float32, least / len(shards), largest / len(shards)))
        factor_of = factor_of * jnp.repeat(draws, extent[dim] // shards_of).reshape([-1 if axis == dim else 1 for axis in range(len(extent))])
    return factor_of


def profile(number_of, total, bound, skew):
    loads = [(1 << 20) // math.isqrt(standing ** skew) + 1 for standing in range(2, number_of + 1)]
    surplus, counts = total - bound - (number_of - 1), [1] * (number_of - 1)
    while surplus > 0:
        candidates = [i for i in range(number_of - 1) if counts[i] < bound]
        whole, left = sum([loads[i] for i in candidates]), surplus
        for i in candidates:
            more = min(bound - counts[i], max(1, left * loads[i] // whole), surplus)
            counts[i] = counts[i] + more
            surplus = surplus - more
    return np.array([bound] + counts)


def uneven(rng, count, total, most, slope):
    if count == 2:
        one = jax.random.randint(rng, (), max(1, total - most), min(most, total - 1) + 1)
        return jnp.stack([one, total - one])
    tallies = jnp.asarray(profile(count, total, most, slope), jnp.int32)
    pairs = (count - 1) // 2
    giver, sink = tallies[1:1 + 2 * pairs:2], tallies[2:2 + 2 * pairs:2]
    slack = jnp.minimum(giver - 1, most - sink)
    passed = jax.random.randint(jax.random.fold_in(rng, 1), (pairs,), 0, 1 << 20) % (slack + 1)
    tallies = tallies.at[1:1 + 2 * pairs:2].set(giver - passed).at[2:2 + 2 * pairs:2].set(sink + passed)
    return tallies[jax.random.permutation(jax.random.fold_in(rng, 2), count)]


def bell_draw(stream_key, shape, width, reach, cuts=(), held_as=jnp.bfloat16):
    result = jax.random.normal(stream_key, shape, jnp.float32) * width
    if len(cuts) > 0:
        result = block_levels(stream_key, shape, cuts, -0.22, 0.18) * result
    return jnp.clip(result, min=-reach, max=reach).astype(held_as)


def setup_inputs(seed: int = 0) -> dict:
    key_list = jax.random.split(jax.random.key(seed), 8)
    queries = draw_queries(jax.random.fold_in(key_list[7], 71), 0)
    key_vectors = draw_key_vectors(jax.random.fold_in(key_list[7], 71), 0)
    value_vectors = bell_draw(key_list[2], (SEQ, KV_HEADS * HEAD_DIM), 1.0, 6.0, ((0, 256),))
    segment_lengths = uneven(key_list[3], SEGMENTS, SEQ, MOST, 1).astype(jnp.int32)
    segment_allowed = draw_segment_allowed(jax.random.fold_in(key_list[7], 71), 0)
    noise_level = touch_ends(jax.random.randint(key_list[5], (SEGMENTS,), 0, LEVELS), jax.random.fold_in(key_list[5], 1), 0, LEVELS - 1).astype(jnp.int32)
    gate_table = jnp.clip(1.0 + 0.18 * jax.random.normal(key_list[6], (LEVELS, HEADS * HEAD_DIM), jnp.float32), 0.099609375, 1.8984375).astype(jnp.bfloat16)
    return {"queries": queries, "key_vectors": key_vectors, "value_vectors": value_vectors, "segment_lengths": segment_lengths, "segment_allowed": segment_allowed, "noise_level": noise_level, "gate_table": gate_table}


NEGATIVE = -1e+30

def segment_labels(segment_lengths):
    segment_ends = jnp.cumsum(segment_lengths).astype(jnp.int32)
    positions = jnp.arange(SEQ, dtype=jnp.int32)
    return lax.optimization_barrier(jnp.sum((segment_ends[None, :] <= positions[:, None]).astype(jnp.int32), axis=1))

def reference(queries, key_vectors, value_vectors, segment_lengths, segment_allowed, noise_level, gate_table):
    labels = segment_labels(segment_lengths)
    group_size = HEADS // KV_HEADS
    key_heads = key_vectors.astype(jnp.float32).reshape(SEQ, KV_HEADS, HEAD_DIM)
    value_heads = value_vectors.astype(jnp.float32).reshape(SEQ, KV_HEADS, HEAD_DIM)
    block_rows = 256

    def one_block(first_row):
        query_block = lax.dynamic_slice_in_dim(queries, first_row, block_rows, 0).astype(jnp.float32)
        query_block = query_block.reshape(block_rows, KV_HEADS, group_size, HEAD_DIM)
        block_labels = lax.dynamic_slice_in_dim(labels, first_row, block_rows, 0)
        visible = segment_allowed[block_labels][:, labels] == 1

        def one_head(head_index):
            scores = jnp.einsum('rqd,kd->qrk', query_block[:, head_index], key_heads[:, head_index]) * (1.0 / math.sqrt(HEAD_DIM))
            scores = jnp.where(visible, scores, NEGATIVE)
            top = lax.optimization_barrier(jnp.max(scores, axis=-1, keepdims=True))
            weights = jnp.where(visible, jnp.exp(scores - top), 0.0)
            totals = lax.optimization_barrier(jnp.sum(weights, axis=-1))
            rounded = lax.optimization_barrier(weights.astype(jnp.bfloat16)).astype(jnp.float32)
            mixed_sum = jnp.einsum('qrk,kd->qrd', rounded, value_heads[:, head_index])
            return mixed_sum / totals[..., None]
        outputs = lax.map(one_head, jnp.arange(KV_HEADS, dtype=jnp.int32))
        outputs = jnp.transpose(outputs, (2, 0, 1, 3)).reshape(block_rows, HEADS * HEAD_DIM)
        gate_rows = gate_table[noise_level[block_labels]].astype(jnp.float32)
        return (outputs * gate_rows).astype(jnp.bfloat16)
    starts = jnp.arange(SEQ // block_rows, dtype=jnp.int32) * block_rows
    return lax.map(one_block, starts).reshape(SEQ, HEADS * HEAD_DIM)
```

```python
import functools
import math

import jax
import jax.numpy as jnp
from jax import lax
from jax.experimental import pallas as pl
from jax.experimental.pallas import tpu as pltpu
from jax.sharding import Mesh, PartitionSpec as P

HEAD_DIM = 128
GROUP = 6
SEGMENTS = 16
AXES = ("zh", "x", "y", "zl", "core")
UNIT = math.log2(math.e) / math.sqrt(HEAD_DIM)
HIDDEN = -1e30
TILE = 256
TILES = 32
STEP = 4
LEAST = 2.0**-60
MOST_SUM = 2.0**100


def shift(x, axis, by):
    return lax.ppermute(x, axis, [(i, (i + by) % 4) for i in range(4)])


def swap(x, axis):
    return lax.ppermute(x, axis, [(0, 1), (1, 0)])


def one_hot_rows(position, bounds_ref):
    inside = (position >= bounds_ref[0:1, :]) & (position < bounds_ref[1:2, :])
    return inside.astype(jnp.float32).astype(jnp.bfloat16)


def attend(
    counts,
    tiles,
    place,
    bounds_ref,
    hidden_ref,
    own_ref,
    other_ref,
    a_refs,
    b_refs,
    kept_ref,
    kept_sums_ref,
    sent_ref,
    sent_sums_ref,
    keys,
    values,
    rows,
    total,
    peak,
    faults,
    arrived,
):
    x, y, zl, core = place[0], place[1], place[2], place[3]
    copies = []

    def bring(source, first_zh, from_x, from_y):
        where = ((from_x % 4) * 4 + from_y % 4) * 2
        for begin, target in ((0, keys), (64, values)):
            copies.append(
                pltpu.make_async_copy(
                    source.at[:, :, pl.ds(begin, 64), :],
                    target.at[pl.ds(first_zh, 2), pl.ds(where, 2), :, pl.ds(0, 128)],
                    arrived,
                )
            )

    away = (0, 3, 1, 2)
    for refs, first_zh, along_x in ((a_refs, 0, True), (b_refs, 2, False)):
        here, minus, plus, far_low, far_high = refs
        for ref, first, step in (
            (here, 0, 0),
            (minus, 0, 3),
            (plus, 0, 1),
            (far_low, 0, 2),
            (far_high, 2, 2),
        ):
            for i in range(ref.shape[0]):
                inner = away[first + i]
                if along_x:
                    bring(ref.at[i], first_zh, x + inner, y + step)
                else:
                    bring(ref.at[i], first_zh, x + step, y + inner)
    for copy in copies:
        copy.start()

    lanes = lax.broadcasted_iota(jnp.int32, (64, 128), 1)
    ones = jnp.ones((32, 64, 128), jnp.bfloat16)
    row = lax.broadcasted_iota(jnp.int32, (32, 64, 128), 1)
    block = lax.broadcasted_iota(jnp.int32, (32, 64, 128), 0)
    for zh in range(4):
        position = zh * 4096 + block * 128 + core * 64 + row
        inside = (position >= bounds_ref[0:1, :][None]) & (position < bounds_ref[1:2, :][None])
        keys[zh, :, :, 128:] = inside.astype(jnp.float32).astype(jnp.bfloat16)
        values[zh, :, :, 128:] = ones
    blank = (lax.broadcasted_iota(jnp.int32, (4, 64, 256), 2) == 255).astype(jnp.float32)
    keys[4, 0:4] = blank.astype(jnp.bfloat16)
    values[4, 0:4] = jnp.zeros((4, 64, 256), jnp.bfloat16)
    faults[...] = jnp.zeros_like(faults)

    for copy in copies:
        copy.wait()

    def prepare(t):
        row = lax.broadcasted_iota(jnp.int32, (64, 128), 0)
        for half, (ref, side) in enumerate(((own_ref, core), (other_ref, 1 - core))):
            position = t * 4096 + (x * 4 + y) * 256 + zl * 128 + side * 64 + row
            mark = jnp.dot(
                one_hot_rows(position, bounds_ref),
                hidden_ref[...],
                preferred_element_type=jnp.float32,
            ).astype(jnp.bfloat16)
            for g in range(GROUP):
                at = pl.ds(half * 384 + g * 64, 64)
                rows[at, 0:128] = ref[t, :, g * 128 : (g + 1) * 128]
                rows[at, 128:256] = mark
        total[...] = jnp.zeros_like(total)

    def load(ref, t, i):
        parts = []
        for j in range(STEP):
            n = tiles[t * TILES + i * STEP + j]
            parts.append(ref[n // 8, pl.ds((n % 8) * 4, 4)].reshape(TILE, 256))
        return jnp.concatenate(parts, axis=0)

    def score(t, i):
        return lax.dot_general(
            rows[...],
            load(keys, t, i),
            (((1,), (1,)), ((), ())),
            preferred_element_type=jnp.float32,
        )

    def finish(t, tops):
        def packed(first, second):
            result = jnp.zeros((64, 128), jnp.float32)
            for g in range(GROUP):
                result = jnp.where(lanes == g, first(g), result)
                if second is not None:
                    result = jnp.where(lanes == 64 + g, second(g), result)
            return result

        for half in range(2):

            def sums(g, half=half):
                return total[half * 384 + g * 64 : half * 384 + (g + 1) * 64, 128:256]

            def top(g, half=half):
                return peak[half * 384 + g * 64 : half * 384 + (g + 1) * 64, :]

            both = packed(sums, top if tops else None)
            if half == 0:
                kept_ref[t] = total[0:384, 0:128]
                kept_sums_ref[t] = both
            else:
                sent_ref[t] = total[384:768, 0:128].astype(jnp.bfloat16)
                sent_sums_ref[t] = both

    def quick(t, _):
        prepare(t)

        def step(i, _):
            weights = jnp.exp2(score(t, i) * UNIT).astype(jnp.bfloat16)
            total[...] += jnp.dot(
                weights, load(values, t, i), preferred_element_type=jnp.float32
            )
            return 0

        lax.fori_loop(0, counts[t], step, 0)
        sums = total[:, 128:256]
        good = (sums >= LEAST) & (sums <= MOST_SUM)
        bad = jnp.where(good, 0.0, 1.0)
        faults[...] = jnp.maximum(faults[...], jnp.max(bad.reshape(96, 8, 128), axis=0))
        finish(t, False)
        return 0

    lax.fori_loop(0, 4, quick, 0)

    @pl.when(jnp.max(faults[...]) > 0.0)
    def _():
        def careful(t, _):
            prepare(t)
            peak[...] = jnp.full_like(peak, -3e38)

            def step(i, _):
                scores = score(t, i) * UNIT
                before = peak[...]
                top = jnp.maximum(before, jnp.max(scores, axis=1, keepdims=True))
                weights = jnp.exp2(scores - top[:, 0:1]).astype(jnp.bfloat16)
                factor = jnp.exp2(before - top)
                added = jnp.dot(
                    weights, load(values, t, i), preferred_element_type=jnp.float32
                )
                total[:, 0:128] = total[:, 0:128] * factor + added[:, 0:128]
                total[:, 128:256] = total[:, 128:256] * factor + added[:, 128:256]
                peak[...] = top
                return 0

            lax.fori_loop(0, counts[t], step, 0)
            finish(t, True)
            return 0

        lax.fori_loop(0, 4, careful, 0)


def attend_call(counts, tiles, place, bounds, hidden, own, other, a_parts, b_parts):
    def body(*refs):
        attend(*refs[:7], refs[7:12], refs[12:17], *refs[17:])

    smem = pl.BlockSpec(memory_space=pltpu.SMEM)
    vmem = pl.BlockSpec(memory_space=pltpu.VMEM)
    anywhere = pl.BlockSpec(memory_space=pl.ANY)
    return pl.pallas_call(
        body,
        out_shape=(
            jax.ShapeDtypeStruct((4, 384, 128), jnp.float32),
            jax.ShapeDtypeStruct((4, 64, 128), jnp.float32),
            jax.ShapeDtypeStruct((4, 384, 128), jnp.bfloat16),
            jax.ShapeDtypeStruct((4, 64, 128), jnp.float32),
        ),
        in_specs=[smem] * 3 + [vmem] * 4 + [anywhere] * 10,
        out_specs=(vmem,) * 4,
        scratch_shapes=[
            pltpu.VMEM((5, 32, 64, 256), jnp.bfloat16),
            pltpu.VMEM((5, 32, 64, 256), jnp.bfloat16),
            pltpu.VMEM((768, 256), jnp.bfloat16),
            pltpu.VMEM((768, 256), jnp.float32),
            pltpu.VMEM((768, 128), jnp.float32),
            pltpu.VMEM((8, 128), jnp.float32),
            pltpu.SemaphoreType.DMA,
        ],
        compiler_params=pltpu.CompilerParams(vmem_limit_bytes=48 * 1024 * 1024),
        name="attend",
    )(counts, tiles, place, bounds, hidden, own, other, *a_parts, *b_parts)


def merge(place, bounds_ref, gate_ref, kept, kept_sums, got, got_sums, out_ref):
    x, y, zl, core = place[0], place[1], place[2], place[3]
    row = lax.broadcasted_iota(jnp.int32, (64, 128), 0)
    for t in range(4):
        position = t * 4096 + (x * 4 + y) * 256 + zl * 128 + core * 64 + row
        gates = jnp.dot(
            one_hot_rows(position, bounds_ref), gate_ref[...], preferred_element_type=jnp.float32
        )
        for g in range(GROUP):
            at = slice(g * 64, (g + 1) * 64)
            first_top = kept_sums[t, :, 64 + g : 65 + g]
            second_top = got_sums[t, :, 64 + g : 65 + g]
            top = jnp.maximum(first_top, second_top)
            first = jnp.exp2(first_top - top)
            second = jnp.exp2(second_top - top)
            sums = first * kept_sums[t, :, g : g + 1] + second * got_sums[t, :, g : g + 1]
            mixed = first * kept[t, at, :] + second * got[t, at, :].astype(jnp.float32)
            result = mixed / sums * gates[:, g * 128 : (g + 1) * 128]
            out_ref[t, :, g * 128 : (g + 1) * 128] = result.astype(jnp.bfloat16)


def merge_call(place, bounds, gate, kept, kept_sums, got, got_sums):
    vmem = pl.BlockSpec(memory_space=pltpu.VMEM)
    return pl.pallas_call(
        merge,
        out_shape=jax.ShapeDtypeStruct((4, 64, 768), jnp.bfloat16),
        in_specs=[pl.BlockSpec(memory_space=pltpu.SMEM)] + [vmem] * 6,
        out_specs=vmem,
        name="merge",
    )(place, bounds, gate, kept, kept_sums, got, got_sums)


def gather_both_ways(own, axis):
    minus = shift(own, axis, 1)
    plus = shift(own, axis, -1)
    half = own.shape[0] // 2
    return minus, plus, shift(minus[:half], axis, 1), shift(plus[half:], axis, -1)


def per_device(
    queries, key_vectors, value_vectors, segment_lengths, segment_allowed, noise_level, gate_table
):
    zh, x, y, zl, core = (lax.axis_index(name) for name in AXES)
    place = jnp.stack([x, y, zl, core, zh]).astype(jnp.int32)

    pairs = jnp.concatenate(
        [
            jnp.transpose(key_vectors.reshape(64, 4, 128), (1, 0, 2)),
            jnp.transpose(value_vectors.reshape(64, 4, 128), (1, 0, 2)),
        ],
        axis=1,
    )
    pairs = jnp.broadcast_to(pairs[:, None], (4, 2, 128, 128)).reshape(8, 128, 128)
    column = lax.all_to_all(pairs, ("zh", "zl"), split_axis=0, concat_axis=0, tiled=True)

    a, b = column[:4], column[4:]
    a_minus, a_plus, a_low, a_high = gather_both_ways(a, "x")
    b_minus, b_plus, b_low, b_high = gather_both_ways(b, "y")
    a_line = jnp.stack([a, a_minus, a_plus, jnp.concatenate([a_low, a_high])])
    b_line = jnp.stack([b, b_minus, b_plus, jnp.concatenate([b_low, b_high])])
    a_parts = (a_line,) + gather_both_ways(a_line, "y")
    b_parts = (b_line,) + gather_both_ways(b_line, "x")
    a_parts = [part.reshape(-1, 2, 2, 128, 128) for part in a_parts]
    b_parts = [part.reshape(-1, 2, 2, 128, 128) for part in b_parts]

    asked = jnp.transpose(queries.reshape(64, 4, 768), (1, 0, 2))
    own = lax.all_to_all(asked, "zh", split_axis=0, concat_axis=0, tiled=True)
    other = swap(own, "core")

    gate_pair = jnp.stack([gate_table, swap(gate_table, "core")])
    gate_all = jnp.concatenate([gate_pair, swap(gate_pair, "zl")])
    gate = lax.dynamic_index_in_dim(gate_all, zh ^ (zl * 2 + core), 0, keepdims=False)
    levels = noise_level[:, None] == jnp.arange(gate.shape[0], dtype=jnp.int32)[None, :]
    levels = jnp.pad(levels.astype(jnp.bfloat16), ((0, 128 - SEGMENTS), (0, 0)))
    gate = jnp.dot(levels, gate, preferred_element_type=jnp.float32).astype(jnp.bfloat16)

    ends = jnp.cumsum(segment_lengths).astype(jnp.int32)
    starts = ends - segment_lengths
    bounds = jnp.pad(jnp.stack([starts, ends]), ((0, 6), (0, 128 - SEGMENTS)))
    hidden = jnp.where(segment_allowed == 1, 0.0, HIDDEN)
    hidden = jnp.pad(hidden, ((0, 128 - SEGMENTS), (0, 128 - SEGMENTS)))
    hidden = jnp.where(jnp.arange(128)[None, :] == 127, HIDDEN, hidden).astype(jnp.bfloat16)
    query_from = jnp.arange(4) * 4096 + (x * 4 + y) * 256 + zl * 128
    key_from = jnp.arange(TILES) * (TILE * 2)
    asks = (starts[None] < query_from[:, None] + 128) & (ends[None] > query_from[:, None])
    holds = (starts[None] < key_from[:, None] + TILE * 2) & (ends[None] > key_from[:, None])
    reach = jnp.any(asks[:, :, None] & (segment_allowed == 1)[None], axis=1)
    seen = jnp.any(reach[:, None, :] & holds[None], axis=2).astype(jnp.int32)
    slot = jnp.cumsum(seen, axis=1) - 1
    wanted = jnp.arange(TILES)
    chosen = (seen[:, :, None] == 1) & (slot[:, :, None] == wanted[None, None])
    tiles = jnp.min(jnp.where(chosen, wanted[None, :, None], TILES), axis=1)
    counts = (jnp.sum(seen, axis=1) + STEP - 1) // STEP
    tiles = tiles.reshape(-1).astype(jnp.int32)
    counts = counts.astype(jnp.int32)

    kept, kept_sums, sent, sent_sums = attend_call(
        counts, tiles, place, bounds, hidden, own, other, a_parts, b_parts
    )
    got, got_sums = swap(sent, "core"), swap(sent_sums, "core")
    merged = merge_call(place, bounds, gate, kept, kept_sums, got, got_sums)
    returned = lax.all_to_all(merged, "zh", split_axis=0, concat_axis=0, tiled=True)
    return jnp.transpose(returned, (1, 0, 2)).reshape(64, 3072)


def solution(mesh):
    finer = Mesh(mesh.devices.reshape(4, 4, 4, 2, 2), AXES)
    by_token = P(AXES, None)
    in_specs = (by_token, by_token, by_token, P(), P(), P(), P(None, ("zl", "core")))
    return jax.shard_map(
        per_device, mesh=finer, in_specs=in_specs, out_specs=by_token, check_vma=False
    )
```

```python
import math

import jax
import jax.numpy as jnp
from jax import lax
from jax.experimental import pallas as pl
from jax.experimental.pallas import tpu as pltpu
from jax.sharding import Mesh, PartitionSpec as P

HEAD_DIM = 128
GROUP = 6
SEGMENTS = 16
AXES = ("zh", "x", "y", "zl", "core")
COLUMN = ("zh", "zl")
UNIT = math.log2(math.e) / math.sqrt(HEAD_DIM)
HIDDEN = -1e30
LEAST = 2.0**-60
MOST_SUM = 2.0**100
TILE = 128
TILES = 64
LONG, SHORT = 8, 4
STAGES = ((0, 16), (16, 32), (48, 16))
LAST = len(STAGES) - 1
AWAY = (0, 3, 1, 2)


def shift(x, axis, by):
    return lax.ppermute(x, axis, [(i, (i + by) % 4) for i in range(4)])


def swap(x, axis):
    return lax.ppermute(x, axis, [(0, 1), (1, 0)])


def shift_cross(x, first, by):
    pairs = []
    for i in range(4):
        for j in range(4):
            for core in range(2):
                along_x = (core == 0) == first
                to = ((i + by) % 4 * 4 + j) if along_x else (i * 4 + (j + by) % 4)
                pairs.append(((i * 4 + j) * 2 + core, to * 2 + core))
    return lax.ppermute(x, ("x", "y", "core"), pairs)


def shift_column(x, by, flip):
    pairs = [(i, (i // 2 + by) % 4 * 2 + (i % 2 ^ flip)) for i in range(8)]
    return lax.ppermute(x, COLUMN, pairs)


def one_hot_rows(position, bounds_ref):
    inside = (position >= bounds_ref[0:1, :]) & (position < bounds_ref[1:2, :])
    return inside.astype(jnp.float32).astype(jnp.bfloat16)


def attend(stage, *refs):
    last = stage == LAST
    base, count = STAGES[stage]
    parts_count = (1, 2, 4)[stage]
    fast_parts = (1, 2, 1)[stage]
    slots, tiles, place, bounds_ref, hidden_ref, own_ref, other_ref = refs[:7]
    refs = refs[7:]
    if stage > 0:
        state_ref, refs = refs[0], refs[1:]
    parts, refs = refs[:parts_count], refs[parts_count:]
    if last:
        kept_ref, kept_sums_ref, sent_ref, refs = *refs[:3], refs[3:]
    else:
        result_ref, refs = refs[0], refs[1:]
    keys, values, marks, ones, rows, total, arrived = refs[:7]
    if last:
        peak, faults = refs[7:]
    x, y, zl, core, zh = place[0], place[1], place[2], place[3], place[4]
    blank_tile = TILES if last else count

    def bring(some, at):
        copies = []
        for part in some:
            n = part.shape[0]
            for begin, target in ((0, keys), (64, values)):
                copies.append(
                    pltpu.make_async_copy(
                        part.at[:, :, pl.ds(begin, 64), :],
                        target.at[pl.ds(at, n)],
                        arrived,
                    )
                )
            at += n
        for copy in copies:
            copy.start()
        return copies

    def mark_keys(first, start, number):
        row = lax.broadcasted_iota(jnp.int32, (TILE, 128), 0)
        inner = ((row // 64) ^ zl) * 128 + core * 64 + row % 64

        def mark(n, _):
            position = tile_from(place, start + n) + inner
            at = first + n
            marks[at] = one_hot_rows(position, bounds_ref)
            return 0

        lax.fori_loop(0, number, mark, 0)

    copies = bring(parts[:fast_parts], 0)
    mark_keys(0, base, count)
    blank = (lax.broadcasted_iota(jnp.int32, (TILE, 128), 1) == 127).astype(jnp.float32)
    marks[blank_tile] = blank.astype(jnp.bfloat16)
    keys[blank_tile] = jnp.zeros((2, 64, 128), jnp.bfloat16)
    values[blank_tile] = jnp.zeros((2, 64, 128), jnp.bfloat16)
    ones[...] = jnp.ones_like(ones)
    if last:
        faults[...] = jnp.zeros_like(faults)
    for copy in copies:
        copy.wait()

    def prepare(t):
        row = lax.broadcasted_iota(jnp.int32, (64, 128), 0)
        for half, (ref, side) in enumerate(((own_ref, core), (other_ref, 1 - core))):
            position = rows_from(place, t) + side * 64 + row
            mark = jnp.dot(
                one_hot_rows(position, bounds_ref),
                hidden_ref[...],
                preferred_element_type=jnp.float32,
            ).astype(jnp.bfloat16)
            for g in range(GROUP):
                at = pl.ds(half * 384 + g * 64, 64)
                rows[at, 0:128] = ref[t, :, g * 128 : (g + 1) * 128]
                rows[at, 128:256] = mark

    def load(ref, beside, numbers):
        wide = [
            jnp.concatenate([ref[n].reshape(TILE, 128), beside(n)], axis=1) for n in numbers
        ]
        return jnp.concatenate(wide, axis=0)

    def load_keys(numbers):
        return load(keys, lambda n: marks[n], numbers)

    def load_values(numbers):
        return load(values, lambda n: ones[...], numbers)

    def score(numbers):
        return lax.dot_general(
            rows[...],
            load_keys(numbers),
            (((1,), (1,)), ((), ())),
            preferred_element_type=jnp.float32,
        )

    def finish(t, tops):
        lanes = lax.broadcasted_iota(jnp.int32, (64, 128), 1)
        for half in range(2):
            both = jnp.zeros((64, 128), jnp.float32)
            for g in range(GROUP):
                at = slice(half * 384 + g * 64, half * 384 + (g + 1) * 64)
                both = jnp.where(lanes == g, total[at, 128:256], both)
                if tops:
                    both = jnp.where(lanes == 64 + g, peak[at, :], both)
            if half == 0:
                kept_ref[t] = total[0:384, 0:128]
                kept_sums_ref[t] = both
            else:
                sent_ref[t, 0:384, :] = total[384:768, 0:128].astype(jnp.bfloat16)
                for i in range(3):
                    piece = both.astype(jnp.bfloat16)
                    sent_ref[t, 384 + 64 * i : 448 + 64 * i, :] = piece
                    both = both - piece.astype(jnp.float32)

    def quick(t, _):
        prepare(t)
        total[...] = jnp.zeros_like(total) if stage == 0 else state_ref[t]
        begin, end = slots[t, base], slots[t, base + count]
        seen = end - begin

        def numbers(first, width):
            picked = []
            for j in range(width):
                inside = first + j < end
                at = jnp.where(inside, first + j, 0)
                picked.append(jnp.where(inside, tiles[t, at] - base, blank_tile))
            return picked

        def add(first, width):
            picked = numbers(first, width)
            weights = jnp.exp2(score(picked) * UNIT).astype(jnp.bfloat16)
            total[...] += jnp.dot(
                weights, load_values(picked), preferred_element_type=jnp.float32
            )

        def step(i, _):
            add(begin + i * LONG, LONG)
            return 0

        whole = (seen + LONG - SHORT - 1) // LONG
        lax.fori_loop(0, whole, step, 0)

        @pl.when(seen > whole * LONG)
        def _():
            add(begin + whole * LONG, SHORT)

        if last:
            sums = total[:, 128:256]
            good = (sums >= LEAST) & (sums <= MOST_SUM)
            bad = jnp.where(good, 0.0, 1.0)
            faults[...] = jnp.maximum(faults[...], jnp.max(bad.reshape(96, 8, 128), axis=0))
            finish(t, False)
        else:
            result_ref[t] = total[...]
        return 0

    lax.fori_loop(0, 4, quick, 0)

    if last:

        @pl.when(jnp.max(faults[...]) > 0.0)
        def _():
            others = bring(parts[fast_parts:], count)
            mark_keys(count, 0, base)
            for copy in others:
                copy.wait()

            def careful(t, _):
                prepare(t)
                total[...] = jnp.zeros_like(total)
                peak[...] = jnp.full_like(peak, -3e38)

                def step(i, _):
                    picked = [i * LONG + j for j in range(LONG)]
                    scores = score(picked) * UNIT
                    before = peak[...]
                    top = jnp.maximum(before, jnp.max(scores, axis=1, keepdims=True))
                    weights = jnp.exp2(scores - top[:, 0:1]).astype(jnp.bfloat16)
                    factor = jnp.exp2(before - top)
                    added = jnp.dot(
                        weights, load_values(picked), preferred_element_type=jnp.float32
                    )
                    total[:, 0:128] = total[:, 0:128] * factor + added[:, 0:128]
                    total[:, 128:256] = total[:, 128:256] * factor + added[:, 128:256]
                    peak[...] = top
                    return 0

                lax.fori_loop(0, TILES // LONG, step, 0)
                finish(t, True)
                return 0

            lax.fori_loop(0, 4, careful, 0)


def attend_call(stage, scalars, tables, asked, state, parts):
    last = stage == LAST
    smem = pl.BlockSpec(memory_space=pltpu.SMEM)
    vmem = pl.BlockSpec(memory_space=pltpu.VMEM)
    anywhere = pl.BlockSpec(memory_space=pl.ANY)
    held = TILES + 1 if last else STAGES[stage][1] + 1
    scratch = [
        pltpu.VMEM((held, 2, 64, 128), jnp.bfloat16),
        pltpu.VMEM((held, 2, 64, 128), jnp.bfloat16),
        pltpu.VMEM((held, TILE, 128), jnp.bfloat16),
        pltpu.VMEM((TILE, 128), jnp.bfloat16),
        pltpu.VMEM((768, 256), jnp.bfloat16),
        pltpu.VMEM((768, 256), jnp.float32),
        pltpu.SemaphoreType.DMA,
    ]
    if last:
        scratch += [pltpu.VMEM((768, 128), jnp.float32), pltpu.VMEM((8, 128), jnp.float32)]
        out_shape = (
            jax.ShapeDtypeStruct((4, 384, 128), jnp.float32),
            jax.ShapeDtypeStruct((4, 64, 128), jnp.float32),
            jax.ShapeDtypeStruct((4, 576, 128), jnp.bfloat16),
        )
    else:
        out_shape = jax.ShapeDtypeStruct((4, 768, 256), jnp.float32)
    states = [] if state is None else [state]

    def body(*refs):
        attend(stage, *refs)

    share = STAGES[stage][1] / TILES
    return pl.pallas_call(
        body,
        out_shape=out_shape,
        in_specs=[smem] * 3 + [vmem] * (4 + len(states)) + [anywhere] * len(parts),
        out_specs=(vmem,) * 3 if last else vmem,
        scratch_shapes=scratch,
        compiler_params=pltpu.CompilerParams(vmem_limit_bytes=24 * 1024 * 1024),
        cost_estimate=pl.CostEstimate(
            flops=int(1.2e10 * share), bytes_accessed=8 << 20, transcendentals=0
        ),
        name=f"attend{stage}",
    )(*scalars, *tables, *asked, *states, *parts)


def ring_step(v):
    return jnp.where(v == 0, 0, jnp.where(v == 1, 3, v - 1))


def tile_from(place, n):
    x, y, core, zh = place[0], place[1], place[3], place[4]
    across, along, depth = ring_step(n // 16), ring_step(n // 4 % 4), n % 4
    first = (core == 0).astype(jnp.int32)
    by_x = along * first + across * (1 - first)
    by_y = across * first + along * (1 - first)
    return (zh + 4 - depth) % 4 * 4096 + ((x + by_x) % 4 * 4 + (y + by_y) % 4) * 256


def rows_from(place, t):
    x, y, zl = place[0], place[1], place[2]
    return t * 4096 + (x * 4 + y) * 256 + zl * 128


def plan(place, lengths, allowed, slots_ref, tiles_ref, bounds_ref, hidden_ref, pad):
    lane = lax.broadcasted_iota(jnp.int32, (8, 128), 1)
    line = lax.broadcasted_iota(jnp.int32, (8, 128), 0)
    bounds = jnp.zeros((8, 128), jnp.int32)
    start = 0
    for c in range(SEGMENTS):
        end = start + lengths[c]
        at = lane == c
        bounds = jnp.where(at & (line == 0), start, bounds)
        bounds = jnp.where(at & (line == 1), end, bounds)
        start = end
    bounds_ref[...] = bounds
    pad[...] = jnp.zeros_like(pad)
    pad[0:SEGMENTS, 0:SEGMENTS] = allowed[...].astype(jnp.float32)
    open_pairs = pad[...]
    row = lax.broadcasted_iota(jnp.int32, (128, 128), 0)
    column = lax.broadcasted_iota(jnp.int32, (128, 128), 1)
    inner = (row < SEGMENTS) & (column < SEGMENTS)
    hides = (inner & (open_pairs < 0.5)) | (column == 127)
    hidden_ref[...] = jnp.where(hides, HIDDEN, 0.0).astype(jnp.bfloat16)

    starts, ends = bounds[0:1, :], bounds[1:2, :]

    def flags(condition):
        return jnp.where(condition, 1.0, 0.0).astype(jnp.bfloat16)

    def dot(a, b, turned):
        return lax.dot_general(
            a, b, (((1,), (1 if turned else 0,)), ((), ())), preferred_element_type=jnp.float32
        )

    query_from = rows_from(place, line)
    asks = (starts < query_from + 128) & (ends > query_from) & (line < 4)
    reach = flags(dot(flags(asks), flags(open_pairs > 0.5), False) > 0.5)
    key_from = tile_from(place, row)
    holds = (starts < key_from + 256) & (ends > key_from) & (row < TILES)
    seen = dot(reach, flags(holds), True) > 0.5
    slots = dot(flags(seen), flags(row < column), False)
    slots_ref[...] = slots.astype(jnp.int32)
    number = lane.astype(jnp.float32).astype(jnp.bfloat16)
    result = jnp.zeros((8, 128), jnp.float32)
    for t in range(4):
        mine = jnp.where(seen[t : t + 1, :], slots[t : t + 1, :], -1.0)
        chosen = flags(mine == row.astype(jnp.float32))
        result = jnp.where(line == t, dot(number, chosen, True), result)
    tiles_ref[...] = result.astype(jnp.int32)


def plan_call(place, lengths, allowed):
    smem = pl.BlockSpec(memory_space=pltpu.SMEM)
    vmem = pl.BlockSpec(memory_space=pltpu.VMEM)
    return pl.pallas_call(
        plan,
        out_shape=(
            jax.ShapeDtypeStruct((8, 128), jnp.int32),
            jax.ShapeDtypeStruct((8, 128), jnp.int32),
            jax.ShapeDtypeStruct((8, 128), jnp.int32),
            jax.ShapeDtypeStruct((128, 128), jnp.bfloat16),
        ),
        in_specs=[smem, smem, vmem],
        out_specs=(vmem,) * 4,
        scratch_shapes=[pltpu.VMEM((128, 128), jnp.float32)],
        compiler_params=pltpu.CompilerParams(vmem_limit_bytes=4 * 1024 * 1024),
        name="plan",
    )(place, lengths, allowed)


def merge(place, bounds_ref, gate_ref, kept, kept_sums, got, *out_refs):
    core, zh = place[3], place[4]
    row = lax.broadcasted_iota(jnp.int32, (64, 128), 0)
    for d, out_ref in enumerate(out_refs):
        t = (zh + d) % 4
        position = rows_from(place, t) + core * 64 + row
        gates = jnp.dot(
            one_hot_rows(position, bounds_ref), gate_ref[...], preferred_element_type=jnp.float32
        )
        near = kept_sums[t]
        far = got[t, 384:448, :].astype(jnp.float32)
        far = far + got[t, 448:512, :].astype(jnp.float32)
        far = far + got[t, 512:576, :].astype(jnp.float32)
        near_top, far_top = pltpu.roll(near, 64, 1), pltpu.roll(far, 64, 1)
        top = jnp.maximum(near_top, far_top)
        near_scale, far_scale = jnp.exp2(near_top - top), jnp.exp2(far_top - top)
        sums = near_scale * near + far_scale * far
        near_scale, far_scale = near_scale / sums, far_scale / sums
        for g in range(GROUP):
            at = slice(g * 64, (g + 1) * 64)
            mixed = near_scale[:, g : g + 1] * kept[t, at, :]
            mixed = mixed + far_scale[:, g : g + 1] * got[t, at, :].astype(jnp.float32)
            result = mixed * gates[:, g * 128 : (g + 1) * 128]
            out_ref[:, g * 128 : (g + 1) * 128] = result.astype(jnp.bfloat16)


def merge_call(place, bounds, gate, kept, kept_sums, got):
    vmem = pl.BlockSpec(memory_space=pltpu.VMEM)
    return pl.pallas_call(
        merge,
        out_shape=(jax.ShapeDtypeStruct((64, 768), jnp.bfloat16),) * 4,
        in_specs=[pl.BlockSpec(memory_space=pltpu.SMEM)] + [vmem] * 5,
        out_specs=(vmem,) * 4,
        compiler_params=pltpu.CompilerParams(vmem_limit_bytes=8 * 1024 * 1024),
        name="merge",
    )(place, bounds, gate, kept, kept_sums, got)


def assemble(place, *refs):
    out_ref = refs[-1]
    for d, ref in enumerate(refs[:-1]):
        head = (place[4] + 4 - d) % 4
        out_ref[:, pl.ds(pl.multiple_of(head * 768, 768), 768)] = ref[...]


def assemble_call(place, pieces):
    vmem = pl.BlockSpec(memory_space=pltpu.VMEM)
    return pl.pallas_call(
        assemble,
        out_shape=jax.ShapeDtypeStruct((64, 3072), jnp.bfloat16),
        in_specs=[pl.BlockSpec(memory_space=pltpu.SMEM)] + [vmem] * 4,
        out_specs=vmem,
        compiler_params=pltpu.CompilerParams(vmem_limit_bytes=4 * 1024 * 1024),
        name="assemble",
    )(place, *pieces)


def per_device(
    queries, key_vectors, value_vectors, segment_lengths, segment_allowed, noise_level, gate_table
):
    zh, x, y, zl, core = (lax.axis_index(name) for name in AXES)
    place = jnp.stack([x, y, zl, core, zh]).astype(jnp.int32)

    asked = jnp.transpose(queries.reshape(64, 4, 768), (1, 0, 2))
    asked, key_vectors, value_vectors = lax.optimization_barrier(
        (asked, key_vectors, value_vectors)
    )
    own = lax.all_to_all(asked, "zh", split_axis=0, concat_axis=0, tiled=True)
    other = swap(own, "core")

    column = []
    for d in range(4):
        at = (zh + d) % 4 * HEAD_DIM
        pair = jnp.concatenate(
            [
                lax.dynamic_slice_in_dim(key_vectors, at, HEAD_DIM, 1),
                lax.dynamic_slice_in_dim(value_vectors, at, HEAD_DIM, 1),
            ],
            axis=0,
        )
        column.append(pair if d == 0 else shift_column(pair, d, 0))
        column.append(shift_column(pair, d, 1))

    own_column = jnp.stack(column)


    own_column, segment_lengths, segment_allowed = lax.optimization_barrier(
        (own_column, segment_lengths, segment_allowed)
    )
    line = jnp.stack([own_column] + [shift_cross(own_column, True, by) for by in (1, -1, 2)])
    line = line.reshape(16, 2, 128, 128)
    slots, tiles, bounds, hidden = plan_call(place, segment_lengths, segment_allowed)
    line, noise_level, gate_table = lax.optimization_barrier((line, noise_level, gate_table))
    near = [shift_cross(line, False, by) for by in (1, -1)]

    gate = lax.ppermute(
        gate_table, ("zh", "zl", "core"), [(b * 4 + h, h * 4 + b) for b in range(4) for h in range(4)]
    )
    levels = noise_level[:, None] == jnp.arange(gate.shape[0], dtype=jnp.int32)[None, :]
    levels = jnp.pad(levels.astype(jnp.bfloat16), ((0, 128 - SEGMENTS), (0, 0)))
    gate = jnp.dot(levels, gate, preferred_element_type=jnp.float32).astype(jnp.bfloat16)

    scalars, tables, asked = (slots, tiles, place), (bounds, hidden), (own, other)
    state = attend_call(0, scalars, tables, asked, None, [line])
    after, near, state, gate = lax.optimization_barrier((line, near, state, gate))
    far = shift_cross(after, False, 2)
    state = attend_call(1, scalars, tables, asked, state, near)
    kept, kept_sums, sent = attend_call(2, scalars, tables, asked, state, [far, line] + near)
    got = swap(sent, "core")
    merged = merge_call(place, bounds, gate, kept, kept_sums, got)
    pieces = [merged[0]] + [shift(merged[d], "zh", d) for d in (1, 2, 3)]
    return assemble_call(place, pieces)


def solution(mesh):
    finer = Mesh(mesh.devices.reshape(4, 4, 4, 2, 2), AXES)
    by_token = P(AXES, None)
    in_specs = (by_token, by_token, by_token, P(), P(), P(), P(None, ("zl", "core")))
    return jax.shard_map(
        per_device, mesh=finer, in_specs=in_specs, out_specs=by_token, check_vma=False
    )
```

```python
import math

import jax
import jax.numpy as jnp
from jax import lax
from jax.experimental import pallas as pl
from jax.experimental.pallas import tpu as pltpu
from jax.sharding import Mesh, PartitionSpec as P

HEAD_DIM = 128
GROUP = 6
SEGMENTS = 16
AXES = ("zh", "x", "y", "zl", "core")
COLUMN = ("zh", "zl")
UNIT = math.log2(math.e) / math.sqrt(HEAD_DIM)
HIDDEN = -1e30
LEAST = 2.0**-60
MOST_SUM = 2.0**100
TILE = 128
TILES = 64
LONG, SHORT = 8, 4
HALF = 8
STAGES = ((0, HALF), (HALF, 48 - HALF), (48, 16))
LAST = len(STAGES) - 1
AWAY = (0, 3, 1, 2)


def shift(x, axis, by):
    return lax.ppermute(x, axis, [(i, (i + by) % 4) for i in range(4)])


def swap(x, axis):
    return lax.ppermute(x, axis, [(0, 1), (1, 0)])


def shift_cross(x, first, by):
    pairs = []
    for i in range(4):
        for j in range(4):
            for core in range(2):
                along_x = (core == 0) == first
                to = ((i + by) % 4 * 4 + j) if along_x else (i * 4 + (j + by) % 4)
                pairs.append(((i * 4 + j) * 2 + core, to * 2 + core))
    return lax.ppermute(x, ("x", "y", "core"), pairs)


def shift_column(x, by, flip):
    pairs = [(i, (i // 2 + by) % 4 * 2 + (i % 2 ^ flip)) for i in range(8)]
    return lax.ppermute(x, COLUMN, pairs)


def one_hot_rows(position, bounds_ref):
    inside = (position >= bounds_ref[0:1, :]) & (position < bounds_ref[1:2, :])
    return inside.astype(jnp.float32).astype(jnp.bfloat16)


def attend(stage, *refs):
    first, last = stage == 0, stage == LAST
    base, count = STAGES[stage]
    parts_count = (1, 3, 4)[stage]
    slots, tiles, marks, row_marks = refs[:4]
    refs = refs[4:]
    if first:
        own_ref, other_ref, refs = refs[0], refs[1], refs[2:]
    else:
        rows, state_ref, refs = refs[0], refs[1], refs[2:]
    parts, refs = refs[:parts_count], refs[parts_count:]
    if first:
        rows, refs = refs[0], refs[1:]
    if last:
        kept_ref, kept_sums_ref, sent_ref, refs = *refs[:3], refs[3:]
    else:
        result_ref, refs = refs[0], refs[1:]
    keys, values, ones, arrived = refs[:4]
    if last:
        total, peak, faults = refs[4:]
    blank_tile = TILES if last else count

    def bring(some, at):
        copies = []
        for part in some:
            n = part.shape[0]
            for begin, target in ((0, keys), (64, values)):
                copies.append(
                    pltpu.make_async_copy(
                        part.at[:, :, pl.ds(begin, 64), :],
                        target.at[pl.ds(at, n)],
                        arrived,
                    )
                )
            at += n
        for copy in copies:
            copy.start()
        return copies

    if first:
        wanted = [parts[0].at[pl.ds(0, HALF)]]
    elif last:
        wanted = parts[:1]
    else:
        wanted = [parts[0].at[pl.ds(HALF, 16 - HALF)]] + list(parts[1:])
    copies = bring(wanted, 0)
    keys[blank_tile] = jnp.zeros((2, 64, 128), jnp.bfloat16)
    values[blank_tile] = jnp.zeros((2, 64, 128), jnp.bfloat16)
    ones[...] = jnp.ones_like(ones)
    if last:
        faults[...] = jnp.zeros_like(faults)
    if first:
        for t in range(4):
            for half, ref in enumerate((own_ref, other_ref)):
                mark = row_marks[t, half]
                for g in range(GROUP):
                    at = pl.ds(half * 384 + g * 64, 64)
                    rows[t, at, 0:128] = ref[t, :, g * 128 : (g + 1) * 128]
                    rows[t, at, 128:256] = mark
    for copy in copies:
        copy.wait()

    def mark_of(n):
        if last:
            n = jnp.where(n < count, n + base, jnp.where(n < TILES, n - count, TILES))
            return marks[n]
        return marks[jnp.where(n < count, n + base, TILES)]

    def load(ref, beside, numbers):
        wide = [
            jnp.concatenate([ref[n].reshape(TILE, 128), beside(n)], axis=1) for n in numbers
        ]
        return jnp.concatenate(wide, axis=0)

    def load_keys(numbers):
        return load(keys, mark_of, numbers)

    def load_values(numbers):
        return load(values, lambda n: ones[...], numbers)

    def score(t, numbers):
        return lax.dot_general(
            rows[t],
            load_keys(numbers),
            (((1,), (1,)), ((), ())),
            preferred_element_type=jnp.float32,
        )

    def finish(t, tops):
        lanes = lax.broadcasted_iota(jnp.int32, (64, 128), 1)
        for half in range(2):
            both = jnp.zeros((64, 128), jnp.float32)
            for g in range(GROUP):
                at = slice(half * 384 + g * 64, half * 384 + (g + 1) * 64)
                both = jnp.where(lanes == g, total[at, 128:256], both)
                if tops:
                    both = jnp.where(lanes == 64 + g, peak[at, :], both)
            if half == 0:
                kept_ref[t] = total[0:384, 0:128]
                kept_sums_ref[t] = both
            else:
                sent_ref[t, 0:384, :] = total[384:768, 0:128].astype(jnp.bfloat16)
                for i in range(3):
                    piece = both.astype(jnp.bfloat16)
                    sent_ref[t, 384 + 64 * i : 448 + 64 * i, :] = piece
                    both = both - piece.astype(jnp.float32)

    def quick(t, _):
        if last:
            total[...] = state_ref[t]
            sum_ref = total
        elif first:
            result_ref[t] = jnp.zeros((768, 256), jnp.float32)
            sum_ref = result_ref.at[t]
        else:
            sum_ref = result_ref.at[t]
        begin, end = slots[t, base], slots[t, base + count]
        seen = end - begin

        def numbers(from_slot, width):
            picked = []
            for j in range(width):
                inside = from_slot + j < end
                at = jnp.where(inside, from_slot + j, 0)
                picked.append(jnp.where(inside, tiles[t, at] - base, blank_tile))
            return picked

        def add(from_slot, width):
            picked = numbers(from_slot, width)
            weights = jnp.exp2(score(t, picked) * UNIT).astype(jnp.bfloat16)
            sum_ref[...] += jnp.dot(
                weights, load_values(picked), preferred_element_type=jnp.float32
            )

        def step(i, _):
            add(begin + i * LONG, LONG)
            return 0

        whole = (seen + LONG - SHORT - 1) // LONG
        lax.fori_loop(0, whole, step, 0)

        @pl.when(seen > whole * LONG)
        def _():
            add(begin + whole * LONG, SHORT)

        if last:
            sums = total[:, 128:256]
            good = (sums >= LEAST) & (sums <= MOST_SUM)
            bad = jnp.where(good, 0.0, 1.0)
            faults[...] = jnp.maximum(faults[...], jnp.max(bad.reshape(96, 8, 128), axis=0))
            finish(t, False)
        return 0

    lax.fori_loop(0, 4, quick, 0)

    if last:

        @pl.when(jnp.max(faults[...]) > 0.0)
        def _():
            others = bring(parts[1:], count)
            for copy in others:
                copy.wait()

            def careful(t, _):
                total[...] = jnp.zeros_like(total)
                peak[...] = jnp.full_like(peak, -3e38)

                def step(i, _):
                    picked = [i * LONG + j for j in range(LONG)]
                    scores = score(t, picked) * UNIT
                    before = peak[...]
                    top = jnp.maximum(before, jnp.max(scores, axis=1, keepdims=True))
                    weights = jnp.exp2(scores - top[:, 0:1]).astype(jnp.bfloat16)
                    factor = jnp.exp2(before - top)
                    added = jnp.dot(
                        weights, load_values(picked), preferred_element_type=jnp.float32
                    )
                    total[:, 0:128] = total[:, 0:128] * factor + added[:, 0:128]
                    total[:, 128:256] = total[:, 128:256] * factor + added[:, 128:256]
                    peak[...] = top
                    return 0

                lax.fori_loop(0, TILES // LONG, step, 0)
                finish(t, True)
                return 0

            lax.fori_loop(0, 4, careful, 0)


def attend_call(stage, lists, tables, asked, state, parts):
    first, last = stage == 0, stage == LAST
    smem = pl.BlockSpec(memory_space=pltpu.SMEM)
    vmem = pl.BlockSpec(memory_space=pltpu.VMEM)
    anywhere = pl.BlockSpec(memory_space=pl.ANY)
    held = TILES + 1 if last else STAGES[stage][1] + 1
    scratch = [
        pltpu.VMEM((held, 2, 64, 128), jnp.bfloat16),
        pltpu.VMEM((held, 2, 64, 128), jnp.bfloat16),
        pltpu.VMEM((TILE, 128), jnp.bfloat16),
        pltpu.SemaphoreType.DMA,
    ]
    state_shape = jax.ShapeDtypeStruct((4, 768, 256), jnp.float32)
    aliases = {}
    if last:
        scratch += [
            pltpu.VMEM((768, 256), jnp.float32),
            pltpu.VMEM((768, 128), jnp.float32),
            pltpu.VMEM((8, 128), jnp.float32),
        ]
        out_shape = (
            jax.ShapeDtypeStruct((4, 384, 128), jnp.float32),
            jax.ShapeDtypeStruct((4, 64, 128), jnp.float32),
            jax.ShapeDtypeStruct((4, 576, 128), jnp.bfloat16),
        )
    elif first:
        out_shape = (jax.ShapeDtypeStruct((4, 768, 256), jnp.bfloat16), state_shape)
    else:
        out_shape = (state_shape,)
        aliases = {5: 0}
    inputs = (*lists, *tables, *(asked if first else state))

    def body(*refs):
        attend(stage, *refs)

    share = STAGES[stage][1] / TILES
    return pl.pallas_call(
        body,
        out_shape=out_shape,
        in_specs=[smem] * 2 + [vmem] * 4 + [anywhere] * len(parts),
        out_specs=(vmem,) * len(out_shape),
        scratch_shapes=scratch,
        input_output_aliases=aliases,
        compiler_params=pltpu.CompilerParams(vmem_limit_bytes=24 * 1024 * 1024),
        cost_estimate=pl.CostEstimate(
            flops=int(1.2e10 * share), bytes_accessed=8 << 20, transcendentals=0
        ),
        name=f"attend{stage}",
    )(*inputs, *parts)


def ring_step(v):
    return jnp.where(v == 0, 0, jnp.where(v == 1, 3, v - 1))


def tile_from(place, n):
    x, y, core, zh = place[0], place[1], place[3], place[4]
    across, along, depth = ring_step(n // 16), ring_step(n // 4 % 4), n % 4
    first = (core == 0).astype(jnp.int32)
    by_x = along * first + across * (1 - first)
    by_y = across * first + along * (1 - first)
    return (zh + 4 - depth) % 4 * 4096 + ((x + by_x) % 4 * 4 + (y + by_y) % 4) * 256


def rows_from(place, t):
    x, y, zl = place[0], place[1], place[2]
    return t * 4096 + (x * 4 + y) * 256 + zl * 128


def plan(place, lengths, allowed, slots_ref, tiles_ref, bounds_ref, marks_ref, row_marks_ref, pad):
    lane = lax.broadcasted_iota(jnp.int32, (8, 128), 1)
    line = lax.broadcasted_iota(jnp.int32, (8, 128), 0)
    bounds = jnp.zeros((8, 128), jnp.int32)
    start = 0
    for c in range(SEGMENTS):
        end = start + lengths[c]
        at = lane == c
        bounds = jnp.where(at & (line == 0), start, bounds)
        bounds = jnp.where(at & (line == 1), end, bounds)
        start = end
    bounds_ref[...] = bounds
    pad[...] = jnp.zeros_like(pad)
    pad[0:SEGMENTS, 0:SEGMENTS] = allowed[...].astype(jnp.float32)
    open_pairs = pad[...]
    row = lax.broadcasted_iota(jnp.int32, (128, 128), 0)
    column = lax.broadcasted_iota(jnp.int32, (128, 128), 1)
    inner = (row < SEGMENTS) & (column < SEGMENTS)
    hides = (inner & (open_pairs < 0.5)) | (column == 127)
    hidden = jnp.where(hides, HIDDEN, 0.0).astype(jnp.bfloat16)

    starts, ends = bounds[0:1, :], bounds[1:2, :]

    def flags(condition):
        return jnp.where(condition, 1.0, 0.0).astype(jnp.bfloat16)

    def dot(a, b, turned):
        return lax.dot_general(
            a, b, (((1,), (1 if turned else 0,)), ((), ())), preferred_element_type=jnp.float32
        )

    query_from = rows_from(place, line)
    asks = (starts < query_from + 128) & (ends > query_from) & (line < 4)
    reach = flags(dot(flags(asks), flags(open_pairs > 0.5), False) > 0.5)
    key_from = tile_from(place, row)
    holds = (starts < key_from + 256) & (ends > key_from) & (row < TILES)
    seen = dot(reach, flags(holds), True) > 0.5
    slots = dot(flags(seen), flags(row < column), False)
    slots_ref[...] = slots.astype(jnp.int32)
    number = lane.astype(jnp.float32).astype(jnp.bfloat16)
    result = jnp.zeros((8, 128), jnp.float32)
    for t in range(4):
        mine = jnp.where(seen[t : t + 1, :], slots[t : t + 1, :], -1.0)
        chosen = flags(mine == row.astype(jnp.float32))
        result = jnp.where(line == t, dot(number, chosen, True), result)
    tiles_ref[...] = result.astype(jnp.int32)

    zl, core = place[2], place[3]
    inner = ((row // 64) ^ zl) * 128 + core * 64 + row % 64

    def mark(n, _):
        marks_ref[n] = one_hot_rows(tile_from(place, n) + inner, bounds)
        return 0

    lax.fori_loop(0, TILES, mark, 0)
    marks_ref[TILES] = flags(column == 127)
    row = lax.broadcasted_iota(jnp.int32, (64, 128), 0)
    for t in range(4):
        for half, side in enumerate((core, 1 - core)):
            position = rows_from(place, t) + side * 64 + row
            mark_row = dot(one_hot_rows(position, bounds), hidden, False)
            row_marks_ref[t, half] = mark_row.astype(jnp.bfloat16)


def plan_call(place, lengths, allowed):
    smem = pl.BlockSpec(memory_space=pltpu.SMEM)
    vmem = pl.BlockSpec(memory_space=pltpu.VMEM)
    return pl.pallas_call(
        plan,
        out_shape=(
            jax.ShapeDtypeStruct((8, 128), jnp.int32),
            jax.ShapeDtypeStruct((8, 128), jnp.int32),
            jax.ShapeDtypeStruct((8, 128), jnp.int32),
            jax.ShapeDtypeStruct((TILES + 1, TILE, 128), jnp.bfloat16),
            jax.ShapeDtypeStruct((4, 2, 64, 128), jnp.bfloat16),
        ),
        in_specs=[smem, smem, vmem],
        out_specs=(vmem,) * 5,
        scratch_shapes=[pltpu.VMEM((128, 128), jnp.float32)],
        compiler_params=pltpu.CompilerParams(vmem_limit_bytes=4 * 1024 * 1024),
        name="plan",
    )(place, lengths, allowed)


def merge(place, bounds_ref, gate_ref, kept, kept_sums, got, *out_refs):
    core, zh = place[3], place[4]
    row = lax.broadcasted_iota(jnp.int32, (64, 128), 0)
    for d, out_ref in enumerate(out_refs):
        t = (zh + d) % 4
        position = rows_from(place, t) + core * 64 + row
        gates = jnp.dot(
            one_hot_rows(position, bounds_ref), gate_ref[...], preferred_element_type=jnp.float32
        )
        near = kept_sums[t]
        far = got[t, 384:448, :].astype(jnp.float32)
        far = far + got[t, 448:512, :].astype(jnp.float32)
        far = far + got[t, 512:576, :].astype(jnp.float32)
        near_top, far_top = pltpu.roll(near, 64, 1), pltpu.roll(far, 64, 1)
        top = jnp.maximum(near_top, far_top)
        near_scale, far_scale = jnp.exp2(near_top - top), jnp.exp2(far_top - top)
        sums = near_scale * near + far_scale * far
        near_scale, far_scale = near_scale / sums, far_scale / sums
        for g in range(GROUP):
            at = slice(g * 64, (g + 1) * 64)
            mixed = near_scale[:, g : g + 1] * kept[t, at, :]
            mixed = mixed + far_scale[:, g : g + 1] * got[t, at, :].astype(jnp.float32)
            result = mixed * gates[:, g * 128 : (g + 1) * 128]
            out_ref[:, g * 128 : (g + 1) * 128] = result.astype(jnp.bfloat16)


def merge_call(place, bounds, gate, kept, kept_sums, got):
    vmem = pl.BlockSpec(memory_space=pltpu.VMEM)
    return pl.pallas_call(
        merge,
        out_shape=(jax.ShapeDtypeStruct((64, 768), jnp.bfloat16),) * 4,
        in_specs=[pl.BlockSpec(memory_space=pltpu.SMEM)] + [vmem] * 5,
        out_specs=(vmem,) * 4,
        compiler_params=pltpu.CompilerParams(vmem_limit_bytes=8 * 1024 * 1024),
        name="merge",
    )(place, bounds, gate, kept, kept_sums, got)


def assemble(place, *refs):
    out_ref = refs[-1]
    for d, ref in enumerate(refs[:-1]):
        head = (place[4] + 4 - d) % 4
        out_ref[:, pl.ds(pl.multiple_of(head * 768, 768), 768)] = ref[...]


def assemble_call(place, pieces):
    vmem = pl.BlockSpec(memory_space=pltpu.VMEM)
    return pl.pallas_call(
        assemble,
        out_shape=jax.ShapeDtypeStruct((64, 3072), jnp.bfloat16),
        in_specs=[pl.BlockSpec(memory_space=pltpu.SMEM)] + [vmem] * 4,
        out_specs=vmem,
        compiler_params=pltpu.CompilerParams(vmem_limit_bytes=4 * 1024 * 1024),
        name="assemble",
    )(place, *pieces)


def per_device(
    queries, key_vectors, value_vectors, segment_lengths, segment_allowed, noise_level, gate_table
):
    zh, x, y, zl, core = (lax.axis_index(name) for name in AXES)
    place = jnp.stack([x, y, zl, core, zh]).astype(jnp.int32)

    column = []
    for d in range(4):
        at = (zh + d) % 4 * HEAD_DIM
        pair = jnp.concatenate(
            [
                lax.dynamic_slice_in_dim(key_vectors, at, HEAD_DIM, 1),
                lax.dynamic_slice_in_dim(value_vectors, at, HEAD_DIM, 1),
            ],
            axis=0,
        )
        column.append(pair if d == 0 else shift_column(pair, d, 0))
        if d > 0:
            column.append(shift_column(pair, d, 1))
        else:
            both = jnp.concatenate([pair, gate_table.reshape(96, 128)], axis=0)
            both = shift_column(both, 0, 1)
            column.append(both[:128])
            gates = jnp.stack([gate_table, both[128:].reshape(16, 768)])

    own_column = jnp.stack(column)

    asked = jnp.transpose(queries.reshape(64, 4, 768), (1, 0, 2))
    own_column, asked = lax.optimization_barrier((own_column, asked))
    own = lax.all_to_all(asked, "zh", split_axis=0, concat_axis=0, tiled=True)


    own_column, segment_lengths, segment_allowed = lax.optimization_barrier(
        (own_column, segment_lengths, segment_allowed)
    )
    line = jnp.stack([own_column] + [shift_cross(own_column, True, by) for by in (1, -1, 2)])
    line = line.reshape(16, 2, 128, 128)
    slots, tiles, bounds, marks, row_marks = plan_call(place, segment_lengths, segment_allowed)
    near = [shift_cross(line, False, by) for by in (1, -1)]

    own, slots, tiles, bounds, marks, row_marks = lax.optimization_barrier(
        (own, slots, tiles, bounds, marks, row_marks)
    )
    other = swap(own, "core")
    own, noise_level, gates = lax.optimization_barrier((own, noise_level, gates))

    swapped = swap(gates, "core")
    which = ((zh // 2) ^ zl) + 2 * ((zh % 2) ^ core)
    gate = lax.dynamic_index_in_dim(jnp.concatenate([gates, swapped]), which, 0, keepdims=False)
    levels = noise_level[:, None] == jnp.arange(gate.shape[0], dtype=jnp.int32)[None, :]
    levels = jnp.pad(levels.astype(jnp.bfloat16), ((0, 128 - SEGMENTS), (0, 0)))
    gate = jnp.dot(levels, gate, preferred_element_type=jnp.float32).astype(jnp.bfloat16)

    lists, tables = (slots, tiles), (marks, row_marks)
    rows, state = attend_call(0, lists, tables, (own, other), None, [line])
    after, near, state, gate = lax.optimization_barrier((line, near, state, gate))
    far = shift_cross(after, False, 2)
    (state,) = attend_call(1, lists, tables, None, (rows, state), [line] + near)
    kept, kept_sums, sent = attend_call(
        2, lists, tables, None, (rows, state), [far, line] + near
    )
    got = swap(sent, "core")
    merged = merge_call(place, bounds, gate, kept, kept_sums, got)
    pieces = [merged[0]] + [shift(merged[d], "zh", d) for d in (1, 2, 3)]
    return assemble_call(place, pieces)


def solution(mesh):
    finer = Mesh(mesh.devices.reshape(4, 4, 4, 2, 2), AXES)
    by_token = P(AXES, None)
    in_specs = (by_token, by_token, by_token, P(), P(), P(), P(None, ("zl", "core")))
    return jax.shard_map(
        per_device, mesh=finer, in_specs=in_specs, out_specs=by_token, check_vma=False
    )
```

```python
import math

import jax
import jax.numpy as jnp
from jax import lax
from jax.experimental import pallas as pl
from jax.experimental.pallas import tpu as pltpu
from jax.sharding import Mesh, PartitionSpec as P

HEAD_DIM = 128
GROUP = 6
SEGMENTS = 16
AXES = ("zh", "x", "y", "zl", "core")
UNIT = math.log2(math.e) / math.sqrt(HEAD_DIM)
HIDDEN = -1e30
LEAST = 2.0**-60
MOST_SUM = 2.0**100
TILE = 128
TILES = 64
LONGEST, LONG, SHORT = 16, 8, 4
HALF = 8
STAGES = ((0, HALF), (HALF, 48 - HALF), (48, 16))
LAST = len(STAGES) - 1
AWAY = (0, 3, 1, 2)


def shift(x, axis, by):
    return lax.ppermute(x, axis, [(i, (i + by) % 4) for i in range(4)])


def swap(x, axis):
    return lax.ppermute(x, axis, [(0, 1), (1, 0)])


def shift_cross(x, first, by):
    pairs = []
    for i in range(4):
        for j in range(4):
            for core in range(2):
                along_x = (core == 0) == first
                to = ((i + by) % 4 * 4 + j) if along_x else (i * 4 + (j + by) % 4)
                pairs.append(((i * 4 + j) * 2 + core, to * 2 + core))
    return lax.ppermute(x, ("x", "y", "core"), pairs)


def one_hot_rows(position, bounds_ref):
    inside = (position >= bounds_ref[0:1, :]) & (position < bounds_ref[1:2, :])
    return inside.astype(jnp.float32).astype(jnp.bfloat16)


def attend(stage, *refs):
    first, last = stage == 0, stage == LAST
    base, count = STAGES[stage]
    parts_count = (1, 3, 4)[stage]
    slots, tiles, marks, row_marks = refs[:4]
    refs = refs[4:]
    if first:
        own_ref, other_ref, refs = refs[0], refs[1], refs[2:]
    else:
        rows, state_ref, refs = refs[0], refs[1], refs[2:]
    parts, refs = refs[:parts_count], refs[parts_count:]
    if first:
        rows, refs = refs[0], refs[1:]
    if last:
        kept_ref, kept_sums_ref, sent_ref, refs = *refs[:3], refs[3:]
    else:
        result_ref, refs = refs[0], refs[1:]
    keys, values, ones, arrived = refs[:4]
    if last:
        total, peak, faults = refs[4:]
    blank_tile = TILES if last else count

    def bring(some, at):
        copies = []
        for part in some:
            n = part.shape[0]
            for begin, target in ((0, keys), (64, values)):
                copies.append(
                    pltpu.make_async_copy(
                        part.at[:, :, pl.ds(begin, 64), :],
                        target.at[pl.ds(at, n)],
                        arrived,
                    )
                )
            at += n
        for copy in copies:
            copy.start()
        return copies

    if first:
        wanted = [parts[0].at[pl.ds(0, HALF)]]
    elif last:
        wanted = parts[:1]
    else:
        wanted = [parts[0].at[pl.ds(HALF, 16 - HALF)]] + list(parts[1:])
    copies = bring(wanted, 0)
    keys[blank_tile] = jnp.zeros((2, 64, 128), jnp.bfloat16)
    values[blank_tile] = jnp.zeros((2, 64, 128), jnp.bfloat16)
    ones[...] = jnp.ones_like(ones)
    if last:
        faults[...] = jnp.zeros_like(faults)
    if first:
        for t in range(4):
            for half, ref in enumerate((own_ref, other_ref)):
                mark = row_marks[t, half]
                for g in range(GROUP):
                    at = pl.ds(half * 384 + g * 64, 64)
                    rows[t, at, 0:128] = ref[t, :, g * 128 : (g + 1) * 128]
                    rows[t, at, 128:256] = mark
    for copy in copies:
        copy.wait()

    def mark_of(n):
        if last:
            n = jnp.where(n < count, n + base, jnp.where(n < TILES, n - count, TILES))
            return marks[n]
        return marks[jnp.where(n < count, n + base, TILES)]

    def load(ref, beside, numbers):
        wide = [
            jnp.concatenate([ref[n].reshape(TILE, 128), beside(n)], axis=1) for n in numbers
        ]
        return jnp.concatenate(wide, axis=0)

    def load_keys(numbers):
        return load(keys, mark_of, numbers)

    def load_values(numbers):
        return load(values, lambda n: ones[...], numbers)

    def score(t, numbers):
        return lax.dot_general(
            rows[t],
            load_keys(numbers),
            (((1,), (1,)), ((), ())),
            preferred_element_type=jnp.float32,
        )

    def finish(t, tops):
        lanes = lax.broadcasted_iota(jnp.int32, (64, 128), 1)
        for half in range(2):
            both = jnp.zeros((64, 128), jnp.float32)
            for g in range(GROUP):
                at = slice(half * 384 + g * 64, half * 384 + (g + 1) * 64)
                both = jnp.where(lanes == g, total[at, 128:256], both)
                if tops:
                    both = jnp.where(lanes == 64 + g, peak[at, :], both)
            if half == 0:
                kept_ref[t] = total[0:384, 0:128]
                kept_sums_ref[t] = both
            else:
                sent_ref[t, 0:384, :] = total[384:768, 0:128].astype(jnp.bfloat16)
                for i in range(3):
                    piece = both.astype(jnp.bfloat16)
                    sent_ref[t, 384 + 64 * i : 448 + 64 * i, :] = piece
                    both = both - piece.astype(jnp.float32)

    def quick(t, _):
        if last:
            total[...] = state_ref[t]
            sum_ref = total
        elif first:
            result_ref[t] = jnp.zeros((768, 256), jnp.float32)
            sum_ref = result_ref.at[t]
        else:
            sum_ref = result_ref.at[t]
        begin, end = slots[t, base], slots[t, base + count]
        seen = end - begin

        def numbers(from_slot, width):
            picked = []
            for j in range(width):
                inside = from_slot + j < end
                at = jnp.where(inside, from_slot + j, 0)
                picked.append(jnp.where(inside, tiles[t, at] - base, blank_tile))
            return picked

        def add(from_slot, width):
            picked = numbers(from_slot, width)
            weights = jnp.exp2(score(t, picked) * UNIT).astype(jnp.bfloat16)
            sum_ref[...] += jnp.dot(
                weights, load_values(picked), preferred_element_type=jnp.float32
            )

        def longest_step(i, _):
            add(begin + i * LONGEST, LONGEST)
            return 0

        longest = seen // LONGEST
        lax.fori_loop(0, longest, longest_step, 0)
        left = seen - longest * LONGEST
        begin = begin + longest * LONGEST

        def step(i, _):
            add(begin + i * LONG, LONG)
            return 0

        whole = (left + LONG - SHORT - 1) // LONG
        lax.fori_loop(0, whole, step, 0)

        @pl.when(left > whole * LONG)
        def _():
            add(begin + whole * LONG, SHORT)

        if last:
            sums = total[:, 128:256]
            good = (sums >= LEAST) & (sums <= MOST_SUM)
            bad = jnp.where(good, 0.0, 1.0)
            faults[...] = jnp.maximum(faults[...], jnp.max(bad.reshape(96, 8, 128), axis=0))
            finish(t, False)
        return 0

    lax.fori_loop(0, 4, quick, 0)

    if last:

        @pl.when(jnp.max(faults[...]) > 0.0)
        def _():
            others = bring(parts[1:], count)
            for copy in others:
                copy.wait()

            def careful(t, _):
                total[...] = jnp.zeros_like(total)
                peak[...] = jnp.full_like(peak, -3e38)

                def step(i, _):
                    picked = [i * LONG + j for j in range(LONG)]
                    scores = score(t, picked) * UNIT
                    before = peak[...]
                    top = jnp.maximum(before, jnp.max(scores, axis=1, keepdims=True))
                    weights = jnp.exp2(scores - top[:, 0:1]).astype(jnp.bfloat16)
                    factor = jnp.exp2(before - top)
                    added = jnp.dot(
                        weights, load_values(picked), preferred_element_type=jnp.float32
                    )
                    total[:, 0:128] = total[:, 0:128] * factor + added[:, 0:128]
                    total[:, 128:256] = total[:, 128:256] * factor + added[:, 128:256]
                    peak[...] = top
                    return 0

                lax.fori_loop(0, TILES // LONG, step, 0)
                finish(t, True)
                return 0

            lax.fori_loop(0, 4, careful, 0)


def attend_call(stage, lists, tables, asked, state, parts):
    first, last = stage == 0, stage == LAST
    smem = pl.BlockSpec(memory_space=pltpu.SMEM)
    vmem = pl.BlockSpec(memory_space=pltpu.VMEM)
    anywhere = pl.BlockSpec(memory_space=pl.ANY)
    held = TILES + 1 if last else STAGES[stage][1] + 1
    scratch = [
        pltpu.VMEM((held, 2, 64, 128), jnp.bfloat16),
        pltpu.VMEM((held, 2, 64, 128), jnp.bfloat16),
        pltpu.VMEM((TILE, 128), jnp.bfloat16),
        pltpu.SemaphoreType.DMA,
    ]
    state_shape = jax.ShapeDtypeStruct((4, 768, 256), jnp.float32)
    aliases = {}
    if last:
        scratch += [
            pltpu.VMEM((768, 256), jnp.float32),
            pltpu.VMEM((768, 128), jnp.float32),
            pltpu.VMEM((8, 128), jnp.float32),
        ]
        out_shape = (
            jax.ShapeDtypeStruct((4, 384, 128), jnp.float32),
            jax.ShapeDtypeStruct((4, 64, 128), jnp.float32),
            jax.ShapeDtypeStruct((4, 576, 128), jnp.bfloat16),
        )
    elif first:
        out_shape = (jax.ShapeDtypeStruct((4, 768, 256), jnp.bfloat16), state_shape)
    else:
        out_shape = (state_shape,)
        aliases = {5: 0}
    inputs = (*lists, *tables, *(asked if first else state))

    def body(*refs):
        attend(stage, *refs)

    share = STAGES[stage][1] / TILES
    return pl.pallas_call(
        body,
        out_shape=out_shape,
        in_specs=[smem] * 2 + [vmem] * 4 + [anywhere] * len(parts),
        out_specs=(vmem,) * len(out_shape),
        scratch_shapes=scratch,
        input_output_aliases=aliases,
        compiler_params=pltpu.CompilerParams(vmem_limit_bytes=24 * 1024 * 1024),
        cost_estimate=pl.CostEstimate(
            flops=int(1.2e10 * share), bytes_accessed=8 << 20, transcendentals=0
        ),
        name=f"attend{stage}",
    )(*inputs, *parts)


def ring_step(v):
    return jnp.where(v == 0, 0, jnp.where(v == 1, 3, v - 1))


def tile_from(place, n):
    x, y, core, zh = place[0], place[1], place[3], place[4]
    across, along, depth = ring_step(n // 16), ring_step(n // 4 % 4), n % 4
    first = (core == 0).astype(jnp.int32)
    by_x = along * first + across * (1 - first)
    by_y = across * first + along * (1 - first)
    return (zh + 4 - depth) % 4 * 4096 + ((x + by_x) % 4 * 4 + (y + by_y) % 4) * 256


def rows_from(place, t):
    x, y, zl = place[0], place[1], place[2]
    return t * 4096 + (x * 4 + y) * 256 + zl * 128


def plan(place, lengths, allowed, slots_ref, tiles_ref, bounds_ref, marks_ref, row_marks_ref, pad):
    lane = lax.broadcasted_iota(jnp.int32, (8, 128), 1)
    line = lax.broadcasted_iota(jnp.int32, (8, 128), 0)
    bounds = jnp.zeros((8, 128), jnp.int32)
    start = 0
    for c in range(SEGMENTS):
        end = start + lengths[c]
        at = lane == c
        bounds = jnp.where(at & (line == 0), start, bounds)
        bounds = jnp.where(at & (line == 1), end, bounds)
        start = end
    bounds_ref[...] = bounds
    pad[...] = jnp.zeros_like(pad)
    pad[0:SEGMENTS, 0:SEGMENTS] = allowed[...].astype(jnp.float32)
    open_pairs = pad[...]
    row = lax.broadcasted_iota(jnp.int32, (128, 128), 0)
    column = lax.broadcasted_iota(jnp.int32, (128, 128), 1)
    inner = (row < SEGMENTS) & (column < SEGMENTS)
    hides = (inner & (open_pairs < 0.5)) | (column == 127)
    hidden = jnp.where(hides, HIDDEN, 0.0).astype(jnp.bfloat16)

    starts, ends = bounds[0:1, :], bounds[1:2, :]

    def flags(condition):
        return jnp.where(condition, 1.0, 0.0).astype(jnp.bfloat16)

    def dot(a, b, turned):
        return lax.dot_general(
            a, b, (((1,), (1 if turned else 0,)), ((), ())), preferred_element_type=jnp.float32
        )

    query_from = rows_from(place, line)
    asks = (starts < query_from + 128) & (ends > query_from) & (line < 4)
    reach = flags(dot(flags(asks), flags(open_pairs > 0.5), False) > 0.5)
    key_from = tile_from(place, row)
    holds = (starts < key_from + 256) & (ends > key_from) & (row < TILES)
    seen = dot(reach, flags(holds), True) > 0.5
    slots = dot(flags(seen), flags(row < column), False)
    slots_ref[...] = slots.astype(jnp.int32)
    number = lane.astype(jnp.float32).astype(jnp.bfloat16)
    result = jnp.zeros((8, 128), jnp.float32)
    for t in range(4):
        mine = jnp.where(seen[t : t + 1, :], slots[t : t + 1, :], -1.0)
        chosen = flags(mine == row.astype(jnp.float32))
        result = jnp.where(line == t, dot(number, chosen, True), result)
    tiles_ref[...] = result.astype(jnp.int32)

    zl, core = place[2], place[3]
    inner = ((row // 64) ^ zl) * 128 + core * 64 + row % 64

    def mark(n, _):
        marks_ref[n] = one_hot_rows(tile_from(place, n) + inner, bounds)
        return 0

    lax.fori_loop(0, TILES, mark, 0)
    marks_ref[TILES] = flags(column == 127)
    row = lax.broadcasted_iota(jnp.int32, (64, 128), 0)
    for t in range(4):
        for half, side in enumerate((core, 1 - core)):
            position = rows_from(place, t) + side * 64 + row
            mark_row = dot(one_hot_rows(position, bounds), hidden, False)
            row_marks_ref[t, half] = mark_row.astype(jnp.bfloat16)


def plan_call(place, lengths, allowed):
    smem = pl.BlockSpec(memory_space=pltpu.SMEM)
    vmem = pl.BlockSpec(memory_space=pltpu.VMEM)
    return pl.pallas_call(
        plan,
        out_shape=(
            jax.ShapeDtypeStruct((8, 128), jnp.int32),
            jax.ShapeDtypeStruct((8, 128), jnp.int32),
            jax.ShapeDtypeStruct((8, 128), jnp.int32),
            jax.ShapeDtypeStruct((TILES + 1, TILE, 128), jnp.bfloat16),
            jax.ShapeDtypeStruct((4, 2, 64, 128), jnp.bfloat16),
        ),
        in_specs=[smem, smem, vmem],
        out_specs=(vmem,) * 5,
        scratch_shapes=[pltpu.VMEM((128, 128), jnp.float32)],
        compiler_params=pltpu.CompilerParams(vmem_limit_bytes=4 * 1024 * 1024),
        name="plan",
    )(place, lengths, allowed)


def merge(place, bounds_ref, gate_ref, kept, kept_sums, got, *out_refs):
    core, zh = place[3], place[4]
    row = lax.broadcasted_iota(jnp.int32, (64, 128), 0)
    for d, out_ref in enumerate(out_refs):
        t = (zh + d) % 4
        position = rows_from(place, t) + core * 64 + row
        gates = jnp.dot(
            one_hot_rows(position, bounds_ref), gate_ref[...], preferred_element_type=jnp.float32
        )
        near = kept_sums[t]
        far = got[t, 384:448, :].astype(jnp.float32)
        far = far + got[t, 448:512, :].astype(jnp.float32)
        far = far + got[t, 512:576, :].astype(jnp.float32)
        near_top, far_top = pltpu.roll(near, 64, 1), pltpu.roll(far, 64, 1)
        top = jnp.maximum(near_top, far_top)
        near_scale, far_scale = jnp.exp2(near_top - top), jnp.exp2(far_top - top)
        sums = near_scale * near + far_scale * far
        near_scale, far_scale = near_scale / sums, far_scale / sums
        for g in range(GROUP):
            at = slice(g * 64, (g + 1) * 64)
            mixed = near_scale[:, g : g + 1] * kept[t, at, :]
            mixed = mixed + far_scale[:, g : g + 1] * got[t, at, :].astype(jnp.float32)
            result = mixed * gates[:, g * 128 : (g + 1) * 128]
            out_ref[:, g * 128 : (g + 1) * 128] = result.astype(jnp.bfloat16)


def merge_call(place, bounds, gate, kept, kept_sums, got):
    vmem = pl.BlockSpec(memory_space=pltpu.VMEM)
    return pl.pallas_call(
        merge,
        out_shape=(jax.ShapeDtypeStruct((64, 768), jnp.bfloat16),) * 4,
        in_specs=[pl.BlockSpec(memory_space=pltpu.SMEM)] + [vmem] * 5,
        out_specs=(vmem,) * 4,
        compiler_params=pltpu.CompilerParams(vmem_limit_bytes=8 * 1024 * 1024),
        name="merge",
    )(place, bounds, gate, kept, kept_sums, got)


def assemble(place, *refs):
    out_ref = refs[-1]
    for d, ref in enumerate(refs[:-1]):
        head = (place[4] + 4 - d) % 4
        out_ref[:, pl.ds(pl.multiple_of(head * 768, 768), 768)] = ref[...]


def assemble_call(place, pieces):
    vmem = pl.BlockSpec(memory_space=pltpu.VMEM)
    return pl.pallas_call(
        assemble,
        out_shape=jax.ShapeDtypeStruct((64, 3072), jnp.bfloat16),
        in_specs=[pl.BlockSpec(memory_space=pltpu.SMEM)] + [vmem] * 4,
        out_specs=vmem,
        compiler_params=pltpu.CompilerParams(vmem_limit_bytes=4 * 1024 * 1024),
        name="assemble",
    )(place, *pieces)


def per_device(
    queries, key_vectors, value_vectors, segment_lengths, segment_allowed, noise_level, gate_table
):
    zh, x, y, zl, core = (lax.axis_index(name) for name in AXES)
    place = jnp.stack([x, y, zl, core, zh]).astype(jnp.int32)

    column = []
    for d in range(4):
        at = (zh + d) % 4 * HEAD_DIM
        pair = jnp.concatenate(
            [
                lax.dynamic_slice_in_dim(key_vectors, at, HEAD_DIM, 1),
                lax.dynamic_slice_in_dim(value_vectors, at, HEAD_DIM, 1),
            ],
            axis=0,
        )
        column.append(pair if d == 0 else shift(pair, "zh", d))
    both = jnp.concatenate(column + [gate_table.reshape(96, 128)], axis=0)
    beside = swap(both, "zl")
    own_column = jnp.stack([both[:512].reshape(4, 128, 128), beside[:512].reshape(4, 128, 128)], 1)
    own_column = own_column.reshape(8, 128, 128)
    gates = jnp.stack([gate_table, beside[512:].reshape(16, 768)])

    asked = jnp.transpose(queries.reshape(64, 4, 768), (1, 0, 2))
    own_column, asked = lax.optimization_barrier((own_column, asked))
    own = lax.all_to_all(asked, "zh", split_axis=0, concat_axis=0, tiled=True)


    own_column, segment_lengths, segment_allowed = lax.optimization_barrier(
        (own_column, segment_lengths, segment_allowed)
    )
    line = jnp.stack([own_column] + [shift_cross(own_column, True, by) for by in (1, -1, 2)])
    line = line.reshape(16, 2, 128, 128)
    slots, tiles, bounds, marks, row_marks = plan_call(place, segment_lengths, segment_allowed)
    near = [shift_cross(line, False, by) for by in (1, -1)]

    own, slots, tiles, bounds, marks, row_marks = lax.optimization_barrier(
        (own, slots, tiles, bounds, marks, row_marks)
    )
    other = swap(own, "core")
    own, noise_level, gates = lax.optimization_barrier((own, noise_level, gates))

    swapped = swap(gates, "core")
    which = ((zh // 2) ^ zl) + 2 * ((zh % 2) ^ core)
    gate = lax.dynamic_index_in_dim(jnp.concatenate([gates, swapped]), which, 0, keepdims=False)
    levels = noise_level[:, None] == jnp.arange(gate.shape[0], dtype=jnp.int32)[None, :]
    levels = jnp.pad(levels.astype(jnp.bfloat16), ((0, 128 - SEGMENTS), (0, 0)))
    gate = jnp.dot(levels, gate, preferred_element_type=jnp.float32).astype(jnp.bfloat16)

    lists, tables = (slots, tiles), (marks, row_marks)
    rows, state = attend_call(0, lists, tables, (own, other), None, [line])
    after, near, state, gate = lax.optimization_barrier((line, near, state, gate))
    far = shift_cross(after, False, 2)
    (state,) = attend_call(1, lists, tables, None, (rows, state), [line] + near)
    kept, kept_sums, sent = attend_call(
        2, lists, tables, None, (rows, state), [far, line] + near
    )
    got = swap(sent, "core")
    merged = merge_call(place, bounds, gate, kept, kept_sums, got)
    pieces = [merged[0]] + [shift(merged[d], "zh", d) for d in (1, 2, 3)]
    return assemble_call(place, pieces)


def solution(mesh):
    finer = Mesh(mesh.devices.reshape(4, 4, 4, 2, 2), AXES)
    by_token = P(AXES, None)
    in_specs = (by_token, by_token, by_token, P(), P(), P(), P(None, ("zl", "core")))
    return jax.shard_map(
        per_device, mesh=finer, in_specs=in_specs, out_specs=by_token, check_vma=False
    )
```

```python
import math

import jax
import jax.numpy as jnp
from jax import lax
from jax.experimental import pallas as pl
from jax.experimental.pallas import tpu as pltpu
from jax.sharding import Mesh, PartitionSpec as P

HEAD_DIM = 128
GROUP = 6
SEGMENTS = 16
AXES = ("zh", "x", "y", "zl", "core")
UNIT = math.log2(math.e) / math.sqrt(HEAD_DIM)
HIDDEN = -1e30
LEAST = 2.0**-60
MOST_SUM = 2.0**100
TILE = 128
TILES = 64
LONGEST, LONG, SHORT = 16, 8, 4
HALF = 8
STAGES = ((0, HALF), (HALF, 48 - HALF), (48, 16))
LAST = len(STAGES) - 1
AWAY = (0, 3, 1, 2)


def shift(x, axis, by):
    return lax.ppermute(x, axis, [(i, (i + by) % 4) for i in range(4)])


def swap(x, axis):
    return lax.ppermute(x, axis, [(0, 1), (1, 0)])


def shift_cross(x, first, by):
    pairs = []
    for i in range(4):
        for j in range(4):
            for core in range(2):
                along_x = (core == 0) == first
                to = ((i + by) % 4 * 4 + j) if along_x else (i * 4 + (j + by) % 4)
                pairs.append(((i * 4 + j) * 2 + core, to * 2 + core))
    return lax.ppermute(x, ("x", "y", "core"), pairs)


def one_hot_rows(position, bounds_ref):
    inside = (position >= bounds_ref[0:1, :]) & (position < bounds_ref[1:2, :])
    return inside.astype(jnp.float32).astype(jnp.bfloat16)


def attend(stage, *refs):
    first, last = stage == 0, stage == LAST
    base, count = STAGES[stage]
    parts_count = (1, 3, 4)[stage]
    slots, tiles, marks, row_marks = refs[:4]
    refs = refs[4:]
    if first:
        own_ref, other_ref, refs = refs[0], refs[1], refs[2:]
    else:
        rows, state_ref, refs = refs[0], refs[1], refs[2:]
    parts, refs = refs[:parts_count], refs[parts_count:]
    if first:
        rows, refs = refs[0], refs[1:]
    if last:
        kept_ref, kept_sums_ref, sent_ref, refs = *refs[:3], refs[3:]
    else:
        result_ref, refs = refs[0], refs[1:]
    keys, values, ones, arrived = refs[:4]
    if last:
        total, peak, faults = refs[4:]
    blank_tile = TILES if last else count

    def bring(some, at):
        copies = []
        for part in some:
            n = part.shape[0]
            for begin, target in ((0, keys), (64, values)):
                copies.append(
                    pltpu.make_async_copy(
                        part.at[:, :, pl.ds(begin, 64), :],
                        target.at[pl.ds(at, n)],
                        arrived,
                    )
                )
            at += n
        for copy in copies:
            copy.start()
        return copies

    if first:
        wanted = [parts[0].at[pl.ds(0, HALF)]]
    elif last:
        wanted = parts[:1]
    else:
        wanted = [parts[0].at[pl.ds(HALF, 16 - HALF)]] + list(parts[1:])
    copies = bring(wanted, 0)
    keys[blank_tile] = jnp.zeros((2, 64, 128), jnp.bfloat16)
    values[blank_tile] = jnp.zeros((2, 64, 128), jnp.bfloat16)
    ones[...] = jnp.ones_like(ones)
    if last:
        faults[...] = jnp.zeros_like(faults)
    if first:
        for t in range(4):
            for half, ref in enumerate((own_ref, other_ref)):
                mark = row_marks[t, half]
                for g in range(GROUP):
                    at = pl.ds(half * 384 + g * 64, 64)
                    rows[t, at, 0:128] = ref[t, :, g * 128 : (g + 1) * 128]
                    rows[t, at, 128:256] = mark
    for copy in copies:
        copy.wait()

    def mark_of(n):
        if last:
            n = jnp.where(n < count, n + base, jnp.where(n < TILES, n - count, TILES))
            return marks[n]
        return marks[jnp.where(n < count, n + base, TILES)]

    def load(ref, beside, numbers):
        wide = [
            jnp.concatenate([ref[n].reshape(TILE, 128), beside(n)], axis=1) for n in numbers
        ]
        return jnp.concatenate(wide, axis=0)

    def load_keys(numbers):
        return load(keys, mark_of, numbers)

    def load_values(numbers):
        return load(values, lambda n: ones[...], numbers)

    def score(t, numbers):
        return lax.dot_general(
            rows[t],
            load_keys(numbers),
            (((1,), (1,)), ((), ())),
            preferred_element_type=jnp.float32,
        )

    def finish(t, tops):
        lanes = lax.broadcasted_iota(jnp.int32, (64, 128), 1)
        for half in range(2):
            both = jnp.zeros((64, 128), jnp.float32)
            for g in range(GROUP):
                at = slice(half * 384 + g * 64, half * 384 + (g + 1) * 64)
                both = jnp.where(lanes == g, total[at, 128:256], both)
                if tops:
                    both = jnp.where(lanes == 64 + g, peak[at, :], both)
            if half == 0:
                kept_ref[t] = total[0:384, 0:128]
                kept_sums_ref[t] = both
            else:
                sent_ref[t, 0:384, :] = total[384:768, 0:128].astype(jnp.bfloat16)
                for i in range(3):
                    piece = both.astype(jnp.bfloat16)
                    sent_ref[t, 384 + 64 * i : 448 + 64 * i, :] = piece
                    both = both - piece.astype(jnp.float32)

    def quick(t, _):
        if last:
            total[...] = state_ref[t]
            sum_ref = total
        elif first:
            result_ref[t] = jnp.zeros((768, 256), jnp.float32)
            sum_ref = result_ref.at[t]
        else:
            sum_ref = result_ref.at[t]
        begin, end = slots[t, base], slots[t, base + count]
        seen = end - begin

        def numbers(from_slot, width):
            picked = []
            for j in range(width):
                inside = from_slot + j < end
                at = jnp.where(inside, from_slot + j, 0)
                picked.append(jnp.where(inside, tiles[t, at] - base, blank_tile))
            return picked

        def add(from_slot, width):
            picked = numbers(from_slot, width)
            weights = jnp.exp2(score(t, picked) * UNIT).astype(jnp.bfloat16)
            sum_ref[...] += jnp.dot(
                weights, load_values(picked), preferred_element_type=jnp.float32
            )

        def longest_step(i, _):
            add(begin + i * LONGEST, LONGEST)
            return 0

        longest = seen // LONGEST
        lax.fori_loop(0, longest, longest_step, 0)
        left = seen - longest * LONGEST
        begin = begin + longest * LONGEST

        def step(i, _):
            add(begin + i * LONG, LONG)
            return 0

        whole = (left + LONG - SHORT - 1) // LONG
        lax.fori_loop(0, whole, step, 0)

        @pl.when(left > whole * LONG)
        def _():
            add(begin + whole * LONG, SHORT)

        if last:
            sums = total[:, 128:256]
            good = (sums >= LEAST) & (sums <= MOST_SUM)
            bad = jnp.where(good, 0.0, 1.0)
            faults[...] = jnp.maximum(faults[...], jnp.max(bad.reshape(96, 8, 128), axis=0))
            finish(t, False)
        return 0

    lax.fori_loop(0, 4, quick, 0)

    if last:

        @pl.when(jnp.max(faults[...]) > 0.0)
        def _():
            others = bring(parts[1:], count)
            for copy in others:
                copy.wait()

            def careful(t, _):
                total[...] = jnp.zeros_like(total)
                peak[...] = jnp.full_like(peak, -3e38)

                def step(i, _):
                    picked = [i * LONG + j for j in range(LONG)]
                    scores = score(t, picked) * UNIT
                    before = peak[...]
                    top = jnp.maximum(before, jnp.max(scores, axis=1, keepdims=True))
                    weights = jnp.exp2(scores - top[:, 0:1]).astype(jnp.bfloat16)
                    factor = jnp.exp2(before - top)
                    added = jnp.dot(
                        weights, load_values(picked), preferred_element_type=jnp.float32
                    )
                    total[:, 0:128] = total[:, 0:128] * factor + added[:, 0:128]
                    total[:, 128:256] = total[:, 128:256] * factor + added[:, 128:256]
                    peak[...] = top
                    return 0

                lax.fori_loop(0, TILES // LONG, step, 0)
                finish(t, True)
                return 0

            lax.fori_loop(0, 4, careful, 0)


def attend_call(stage, lists, tables, asked, state, parts):
    first, last = stage == 0, stage == LAST
    smem = pl.BlockSpec(memory_space=pltpu.SMEM)
    vmem = pl.BlockSpec(memory_space=pltpu.VMEM)
    anywhere = pl.BlockSpec(memory_space=pl.ANY)
    held = TILES + 1 if last else STAGES[stage][1] + 1
    scratch = [
        pltpu.VMEM((held, 2, 64, 128), jnp.bfloat16),
        pltpu.VMEM((held, 2, 64, 128), jnp.bfloat16),
        pltpu.VMEM((TILE, 128), jnp.bfloat16),
        pltpu.SemaphoreType.DMA,
    ]
    state_shape = jax.ShapeDtypeStruct((4, 768, 256), jnp.float32)
    aliases = {}
    if last:
        scratch += [
            pltpu.VMEM((768, 256), jnp.float32),
            pltpu.VMEM((768, 128), jnp.float32),
            pltpu.VMEM((8, 128), jnp.float32),
        ]
        out_shape = (
            jax.ShapeDtypeStruct((4, 384, 128), jnp.float32),
            jax.ShapeDtypeStruct((4, 64, 128), jnp.float32),
            jax.ShapeDtypeStruct((4, 576, 128), jnp.bfloat16),
        )
    elif first:
        out_shape = (jax.ShapeDtypeStruct((4, 768, 256), jnp.bfloat16), state_shape)
    else:
        out_shape = (state_shape,)
        aliases = {5: 0}
    inputs = (*lists, *tables, *(asked if first else state))

    def body(*refs):
        attend(stage, *refs)

    share = STAGES[stage][1] / TILES
    return pl.pallas_call(
        body,
        out_shape=out_shape,
        in_specs=[smem] * 2 + [vmem] * 4 + [anywhere] * len(parts),
        out_specs=(vmem,) * len(out_shape),
        scratch_shapes=scratch,
        input_output_aliases=aliases,
        compiler_params=pltpu.CompilerParams(vmem_limit_bytes=24 * 1024 * 1024),
        cost_estimate=pl.CostEstimate(
            flops=int(1.2e10 * share), bytes_accessed=8 << 20, transcendentals=0
        ),
        name=f"attend{stage}",
    )(*inputs, *parts)


def ring_step(v):
    return jnp.where(v == 0, 0, jnp.where(v == 1, 3, v - 1))


def tile_from(place, n):
    x, y, core, zh = place[0], place[1], place[3], place[4]
    across, along, depth = ring_step(n // 16), ring_step(n // 4 % 4), n % 4
    first = (core == 0).astype(jnp.int32)
    by_x = along * first + across * (1 - first)
    by_y = across * first + along * (1 - first)
    return (zh + 4 - depth) % 4 * 4096 + ((x + by_x) % 4 * 4 + (y + by_y) % 4) * 256


def rows_from(place, t):
    x, y, zl = place[0], place[1], place[2]
    return t * 4096 + (x * 4 + y) * 256 + zl * 128


def plan(place, lengths, allowed, slots_ref, tiles_ref, bounds_ref, marks_ref, row_marks_ref, pad):
    lane = lax.broadcasted_iota(jnp.int32, (8, 128), 1)
    line = lax.broadcasted_iota(jnp.int32, (8, 128), 0)
    bounds = jnp.zeros((8, 128), jnp.int32)
    start = 0
    for c in range(SEGMENTS):
        end = start + lengths[c]
        at = lane == c
        bounds = jnp.where(at & (line == 0), start, bounds)
        bounds = jnp.where(at & (line == 1), end, bounds)
        start = end
    bounds_ref[...] = bounds
    pad[...] = jnp.zeros_like(pad)
    pad[0:SEGMENTS, 0:SEGMENTS] = allowed[...].astype(jnp.float32)
    open_pairs = pad[...]
    row = lax.broadcasted_iota(jnp.int32, (128, 128), 0)
    column = lax.broadcasted_iota(jnp.int32, (128, 128), 1)
    inner = (row < SEGMENTS) & (column < SEGMENTS)
    hides = (inner & (open_pairs < 0.5)) | (column == 127)
    hidden = jnp.where(hides, HIDDEN, 0.0).astype(jnp.bfloat16)

    starts, ends = bounds[0:1, :], bounds[1:2, :]

    def flags(condition):
        return jnp.where(condition, 1.0, 0.0).astype(jnp.bfloat16)

    def dot(a, b, turned):
        return lax.dot_general(
            a, b, (((1,), (1 if turned else 0,)), ((), ())), preferred_element_type=jnp.float32
        )

    query_from = rows_from(place, line)
    asks = (starts < query_from + 128) & (ends > query_from) & (line < 4)
    reach = flags(dot(flags(asks), flags(open_pairs > 0.5), False) > 0.5)
    key_from = tile_from(place, row)
    holds = (starts < key_from + 256) & (ends > key_from) & (row < TILES)
    seen = dot(reach, flags(holds), True) > 0.5
    slots = dot(flags(seen), flags(row < column), False)
    slots_ref[...] = slots.astype(jnp.int32)
    number = lane.astype(jnp.float32).astype(jnp.bfloat16)
    result = jnp.zeros((8, 128), jnp.float32)
    for t in range(4):
        mine = jnp.where(seen[t : t + 1, :], slots[t : t + 1, :], -1.0)
        chosen = flags(mine == row.astype(jnp.float32))
        result = jnp.where(line == t, dot(number, chosen, True), result)
    tiles_ref[...] = result.astype(jnp.int32)

    zl, core = place[2], place[3]
    inner = ((row // 64) ^ zl) * 128 + core * 64 + row % 64

    def mark(n, _):
        marks_ref[n] = one_hot_rows(tile_from(place, n) + inner, bounds)
        return 0

    lax.fori_loop(0, TILES, mark, 0)
    marks_ref[TILES] = flags(column == 127)
    row = lax.broadcasted_iota(jnp.int32, (64, 128), 0)
    for t in range(4):
        for half, side in enumerate((core, 1 - core)):
            position = rows_from(place, t) + side * 64 + row
            mark_row = dot(one_hot_rows(position, bounds), hidden, False)
            row_marks_ref[t, half] = mark_row.astype(jnp.bfloat16)


def plan_call(place, lengths, allowed):
    smem = pl.BlockSpec(memory_space=pltpu.SMEM)
    vmem = pl.BlockSpec(memory_space=pltpu.VMEM)
    return pl.pallas_call(
        plan,
        out_shape=(
            jax.ShapeDtypeStruct((8, 128), jnp.int32),
            jax.ShapeDtypeStruct((8, 128), jnp.int32),
            jax.ShapeDtypeStruct((8, 128), jnp.int32),
            jax.ShapeDtypeStruct((TILES + 1, TILE, 128), jnp.bfloat16),
            jax.ShapeDtypeStruct((4, 2, 64, 128), jnp.bfloat16),
        ),
        in_specs=[smem, smem, vmem],
        out_specs=(vmem,) * 5,
        scratch_shapes=[pltpu.VMEM((128, 128), jnp.float32)],
        compiler_params=pltpu.CompilerParams(vmem_limit_bytes=4 * 1024 * 1024),
        name="plan",
    )(place, lengths, allowed)


def merge(place, bounds_ref, gate_ref, kept, kept_sums, got, *out_refs):
    core, zh = place[3], place[4]
    row = lax.broadcasted_iota(jnp.int32, (64, 128), 0)
    for d, out_ref in enumerate(out_refs):
        t = (zh + d) % 4
        position = rows_from(place, t) + core * 64 + row
        gates = jnp.dot(
            one_hot_rows(position, bounds_ref), gate_ref[...], preferred_element_type=jnp.float32
        )
        near = kept_sums[t]
        far = got[t, 384:448, :].astype(jnp.float32)
        far = far + got[t, 448:512, :].astype(jnp.float32)
        far = far + got[t, 512:576, :].astype(jnp.float32)
        near_top, far_top = pltpu.roll(near, 64, 1), pltpu.roll(far, 64, 1)
        top = jnp.maximum(near_top, far_top)
        near_scale, far_scale = jnp.exp2(near_top - top), jnp.exp2(far_top - top)
        sums = near_scale * near + far_scale * far
        near_scale, far_scale = near_scale / sums, far_scale / sums
        for g in range(GROUP):
            at = slice(g * 64, (g + 1) * 64)
            mixed = near_scale[:, g : g + 1] * kept[t, at, :]
            mixed = mixed + far_scale[:, g : g + 1] * got[t, at, :].astype(jnp.float32)
            result = mixed * gates[:, g * 128 : (g + 1) * 128]
            out_ref[:, g * 128 : (g + 1) * 128] = result.astype(jnp.bfloat16)


def merge_call(place, bounds, gate, kept, kept_sums, got):
    vmem = pl.BlockSpec(memory_space=pltpu.VMEM)
    return pl.pallas_call(
        merge,
        out_shape=(jax.ShapeDtypeStruct((64, 768), jnp.bfloat16),) * 4,
        in_specs=[pl.BlockSpec(memory_space=pltpu.SMEM)] + [vmem] * 5,
        out_specs=(vmem,) * 4,
        compiler_params=pltpu.CompilerParams(vmem_limit_bytes=8 * 1024 * 1024),
        name="merge",
    )(place, bounds, gate, kept, kept_sums, got)


def assemble(place, *refs):
    out_ref = refs[-1]
    for d, ref in enumerate(refs[:-1]):
        head = (place[4] + 4 - d) % 4
        out_ref[:, pl.ds(pl.multiple_of(head * 768, 768), 768)] = ref[...]


def assemble_call(place, pieces):
    vmem = pl.BlockSpec(memory_space=pltpu.VMEM)
    return pl.pallas_call(
        assemble,
        out_shape=jax.ShapeDtypeStruct((64, 3072), jnp.bfloat16),
        in_specs=[pl.BlockSpec(memory_space=pltpu.SMEM)] + [vmem] * 4,
        out_specs=vmem,
        compiler_params=pltpu.CompilerParams(vmem_limit_bytes=4 * 1024 * 1024),
        name="assemble",
    )(place, *pieces)


def per_device(
    queries, key_vectors, value_vectors, segment_lengths, segment_allowed, noise_level, gate_table
):
    zh, x, y, zl, core = (lax.axis_index(name) for name in AXES)
    place = jnp.stack([x, y, zl, core, zh]).astype(jnp.int32)

    column = []
    for d in range(4):
        at = (zh + d) % 4 * HEAD_DIM
        pair = jnp.concatenate(
            [
                lax.dynamic_slice_in_dim(key_vectors, at, HEAD_DIM, 1),
                lax.dynamic_slice_in_dim(value_vectors, at, HEAD_DIM, 1),
            ],
            axis=0,
        )
        column.append(pair if d == 0 else shift(pair, "zh", d))
    gate_table, _ = lax.optimization_barrier((gate_table, column[1]))
    both = jnp.concatenate(column + [gate_table.reshape(96, 128)], axis=0)
    beside = swap(both, "zl")
    own_column = jnp.stack([both[:512].reshape(4, 128, 128), beside[:512].reshape(4, 128, 128)], 1)
    own_column = own_column.reshape(8, 128, 128)
    gates = jnp.stack([gate_table, beside[512:].reshape(16, 768)])

    asked = jnp.transpose(queries.reshape(64, 4, 768), (1, 0, 2))
    own_column, asked = lax.optimization_barrier((own_column, asked))
    own = lax.all_to_all(asked, "zh", split_axis=0, concat_axis=0, tiled=True)


    own_column, segment_lengths, segment_allowed = lax.optimization_barrier(
        (own_column, segment_lengths, segment_allowed)
    )
    line = jnp.stack([own_column] + [shift_cross(own_column, True, by) for by in (1, -1, 2)])
    line = line.reshape(16, 2, 128, 128)
    slots, tiles, bounds, marks, row_marks = plan_call(place, segment_lengths, segment_allowed)
    near = [shift_cross(line, False, by) for by in (1, -1)]

    own, slots, tiles, bounds, marks, row_marks = lax.optimization_barrier(
        (own, slots, tiles, bounds, marks, row_marks)
    )
    other = swap(own, "core")
    own, noise_level, gates = lax.optimization_barrier((own, noise_level, gates))

    swapped = swap(gates, "core")
    which = ((zh // 2) ^ zl) + 2 * ((zh % 2) ^ core)
    gate = lax.dynamic_index_in_dim(jnp.concatenate([gates, swapped]), which, 0, keepdims=False)
    levels = noise_level[:, None] == jnp.arange(gate.shape[0], dtype=jnp.int32)[None, :]
    levels = jnp.pad(levels.astype(jnp.bfloat16), ((0, 128 - SEGMENTS), (0, 0)))
    gate = jnp.dot(levels, gate, preferred_element_type=jnp.float32).astype(jnp.bfloat16)

    lists, tables = (slots, tiles), (marks, row_marks)
    rows, state = attend_call(0, lists, tables, (own, other), None, [line])
    after, near, state, gate = lax.optimization_barrier((line, near, state, gate))
    far = shift_cross(after, False, 2)
    (state,) = attend_call(1, lists, tables, None, (rows, state), [line] + near)
    kept, kept_sums, sent = attend_call(
        2, lists, tables, None, (rows, state), [far, line] + near
    )
    got = swap(sent, "core")
    merged = merge_call(place, bounds, gate, kept, kept_sums, got)
    pieces = [merged[0]] + [shift(merged[d], "zh", d) for d in (1, 2, 3)]
    return assemble_call(place, pieces)


def solution(mesh):
    finer = Mesh(mesh.devices.reshape(4, 4, 4, 2, 2), AXES)
    by_token = P(AXES, None)
    in_specs = (by_token, by_token, by_token, P(), P(), P(), P(None, ("zl", "core")))
    return jax.shard_map(
        per_device, mesh=finer, in_specs=in_specs, out_specs=by_token, check_vma=False
    )
```
